128 devices in a mesh: pipe: 4 (over x), ctx: 16 (over z, y), tp: 2 (over core).
Axes of the slice: x: 4, y: 4, z: 4, core: 2. Of those that a mesh axis runs over, the one named last changes fastest.
Arguments:
- queries: bfloat16 [4, 2048, 4096], P('pipe', 'ctx', 'tp'), may hold values from -12 to 12
- forget_logits: bfloat16 [4, 2048, 4096], P('pipe', 'ctx', 'tp'), may hold values from -1 to 12
- values: bfloat16 [4, 2048, 4096], P('pipe', 'ctx', 'tp'), may hold values from -48 to 48
- gates: bfloat16 [4, 2048, 4096], P('pipe', 'ctx', 'tp'), may hold values from -6 to 6
- output_grad: bfloat16 [4, 2048, 4096], P('pipe', 'ctx', 'tp'), may hold values from -6 to 6
- lower_bound: float32 [4, 4096], P('pipe', 'tp'), may hold values from 0.45 to 0.7
- norm_gain: float32 [4, 4096], P('pipe', 'tp'), may hold values from 0.5 to 2
Outputs:
- handed_query_grad: bfloat16 [4, 2048, 4096], P('pipe', 'ctx', 'tp')
- handed_logit_grad: bfloat16 [4, 2048, 4096], P('pipe', 'ctx', 'tp')
- handed_value_grad: bfloat16 [4, 2048, 4096], P('pipe', 'ctx', 'tp')
- handed_gate_grad: bfloat16 [4, 2048, 4096], P('pipe', 'ctx', 'tp')
The draws below stay inside these ranges and needn't reach their ends.
All inputs are finite; a program needn't handle non-finite values.
Results may differ from the reference program's by a relative error of at most 0.0024.
Values may be sent and summed in bfloat16 or wider, within the bound.
No kernel may reach another device: no remote copies, remote signals or barrier semaphores. Data moves between devices by JAX's collectives and lax.ppermute only.
A program may use at most 128 MiB of HBM per device.

```python
import math
import jax
import jax.numpy as jnp
from jax import lax

HEADS = 32
DK = 128
BLOCK = 128
GROUP = 128
CASCADE_PARTS = 4
SEQUENCE_LENGTH = 2048
HEAD_COLUMNS = 4096


def draw_queries(key, part):
    key = jax.random.fold_in(key, 11)
    first, second = jax.random.split(key, 2)
    base = jnp.clip(jax.random.normal(first, (CASCADE_PARTS, SEQUENCE_LENGTH, HEAD_COLUMNS), jnp.float32), -4.0, 4.0)
    scales = jnp.exp(jax.random.uniform(second, (CASCADE_PARTS, SEQUENCE_LENGTH, 1), jnp.float32, math.log(0.3), math.log(3.0)))
    return (base * scales).astype(jnp.bfloat16)


def draw_forget_logits(key, part):
    key = jax.random.fold_in(key, 23)
    key_matrix = jax.random.split(key, 7)
    fast_share = 0.5
    fast_heads = jax.random.bernoulli(key_matrix[0], fast_share, (CASCADE_PARTS, 1, 1, HEADS, 1))
    fast_base = jax.random.uniform(key_matrix[1], (CASCADE_PARTS, 1, 1, HEADS, DK), jnp.float32, 2.0, 3.5)
    slow_base = math.log(SEQUENCE_LENGTH) + jax.random.uniform(key_matrix[2], (CASCADE_PARTS, 1, 1, HEADS, DK), jnp.float32, 0.0, 1.0)
    base_level = jnp.where(fast_heads, fast_base, slow_base)
    noise = jax.random.uniform(key_matrix[3], (CASCADE_PARTS, SEQUENCE_LENGTH // GROUP, GROUP, HEADS, DK), jnp.float32, -0.35, 0.35)
    offset = jax.random.uniform(key_matrix[4], (CASCADE_PARTS, SEQUENCE_LENGTH // GROUP, 1, HEADS, 1), jnp.float32, -0.35, 0.35)
    stable_decay = (base_level + noise + offset).reshape(CASCADE_PARTS, SEQUENCE_LENGTH, HEAD_COLUMNS)
    spike_locations = jax.random.randint(key_matrix[5], (CASCADE_PARTS, 1, 3), 0, SEQUENCE_LENGTH)
    position_index = jax.lax.broadcasted_iota(jnp.int32, (CASCADE_PARTS, SEQUENCE_LENGTH, 3), 1)
    spiking_flags = jnp.any(position_index == spike_locations, axis=2)[:, :, None]
    spike_threshold = jax.random.uniform(key_matrix[6], (CASCADE_PARTS, SEQUENCE_LENGTH, HEAD_COLUMNS), jnp.float32, -1.0, -0.3)
    return jnp.where(spiking_flags, spike_threshold, stable_decay).astype(jnp.bfloat16)


def draw_values(key, part):
    key = jax.random.fold_in(key, 37)
    first, second, third = jax.random.split(key, 3)
    columns = jax.lax.broadcasted_iota(jnp.float32, (1, 1, HEAD_COLUMNS), 2)
    rising = jnp.exp(math.log(3.0) * columns / (HEAD_COLUMNS - 1))
    column_scale = rising * jnp.exp(jax.random.uniform(second, (CASCADE_PARTS, 1, HEAD_COLUMNS), jnp.float32, math.log(0.6), math.log(2.0)))
    row_scale = jnp.exp(jax.random.uniform(third, (CASCADE_PARTS, SEQUENCE_LENGTH, 1), jnp.float32, math.log(0.5), math.log(2.0)))
    base = jnp.clip(jax.random.normal(first, (CASCADE_PARTS, SEQUENCE_LENGTH, HEAD_COLUMNS), jnp.float32), -4.0, 4.0)
    return (base * column_scale * row_scale).astype(jnp.bfloat16)


def level_of(stream_key, extent, cuts, smallest, high):
    def one(position, parts):
        heights = jax.random.uniform(jax.random.fold_in(jax.random.fold_in(stream_key, 6), position), (parts,), jnp.float32, smallest / len(cuts), high / len(cuts))
        return jnp.repeat(jnp.exp(heights), extent[position] // parts).reshape((-1,) + (1,) * (len(extent) - position - 1))

    level = one(*cuts[0])
    for cut in cuts[1:]:
        level = level * one(*cut)
    return level


def scatter_about(rng, dims, spread, most, shards=(), held_as=jnp.bfloat16):
    array = jax.random.normal(rng, dims, jnp.float32) * spread
    if len(shards) > 0:
        array = level_of(rng, dims, shards, -0.22, 0.18) * array
    return jnp.clip(array, min=-most, max=most).astype(held_as)


def setup_inputs(seed: int = 0) -> dict:
    arg_keys = jax.random.split(jax.random.key(seed), 8)
    queries = draw_queries(jax.random.fold_in(arg_keys[7], 71), 0)
    forget_logits = draw_forget_logits(jax.random.fold_in(arg_keys[7], 71), 0)
    values = draw_values(jax.random.fold_in(arg_keys[7], 71), 0)
    gates = scatter_about(arg_keys[3], (CASCADE_PARTS, SEQUENCE_LENGTH, HEAD_COLUMNS), 1.0, 6.0, ((0, 4), (1, 16), (2, 2)))
    output_grad = scatter_about(arg_keys[4], (CASCADE_PARTS, SEQUENCE_LENGTH, HEAD_COLUMNS), 1.0, 6.0, ((0, 4), (1, 16), (2, 2)))
    lower_bound = jnp.clip(0.45 + 0.25 * jax.random.uniform(arg_keys[5], (CASCADE_PARTS, HEAD_COLUMNS), jnp.float32) ** level_of(arg_keys[5], (CASCADE_PARTS, HEAD_COLUMNS), ((0, 4), (1, 2)), -0.2, 0.2), 0.45, 0.7)
    norm_gain = jnp.clip(jnp.exp(math.log(2.0) - 1.3862944 * jax.random.uniform(arg_keys[6], (CASCADE_PARTS, HEAD_COLUMNS), jnp.float32) ** level_of(arg_keys[6], (CASCADE_PARTS, HEAD_COLUMNS), ((0, 4), (1, 2)), -0.2, 0.2)), 0.5, 2.0)
    return dict(queries=queries, forget_logits=forget_logits, values=values, gates=gates, output_grad=output_grad, lower_bound=lower_bound, norm_gain=norm_gain)


exact_arithmetic_mode = lax.Precision.HIGHEST
epsilon = 1e-06

def causal_mask(length):
    row_index = lax.broadcasted_iota(jnp.int32, (length, length), 0)
    col_index = lax.broadcasted_iota(jnp.int32, (length, length), 1)
    return row_index >= col_index

def block_forward(incoming_memory, pieces):
    query_block, key_block, value_tile, log_forget = pieces
    running_total = jnp.cumsum(log_forget, axis=0)
    final_cumulative_forgetting = running_total[-1]
    probe_vector_scaled = query_block * jnp.exp(running_total)
    key_rescaled = key_block * jnp.exp(-running_total)
    lookup_vector_leftover = key_block * jnp.exp(final_cumulative_forgetting[None] - running_total)
    similarity_weights = jnp.einsum('thk,shk->hts', probe_vector_scaled, key_rescaled, precision=exact_arithmetic_mode)
    similarity_weights = jnp.where(causal_mask(query_block.shape[0])[None], similarity_weights, 0.0)
    within = jnp.einsum('hts,shv->thv', similarity_weights, value_tile, precision=exact_arithmetic_mode)
    across_heads = jnp.einsum('ubl,bli->ubi', probe_vector_scaled, incoming_memory, precision=exact_arithmetic_mode)
    fresh_state = jnp.einsum('ycw,yco->cwo', lookup_vector_leftover, value_tile, precision=exact_arithmetic_mode)
    revised_memory = jnp.exp(final_cumulative_forgetting)[:, :, None] * incoming_memory + fresh_state
    return (revised_memory, (within + across_heads, incoming_memory))

def block_backward(incoming_memory, pieces):
    query_block, key_block, value_tile, log_forget, result_derivative_piece, initial_state = pieces
    running_total = jnp.cumsum(log_forget, axis=0)
    final_cumulative_forgetting = running_total[-1]
    probe_vector_scaled = query_block * jnp.exp(running_total)
    key_rescaled = key_block * jnp.exp(-running_total)
    lookup_vector_leftover = key_block * jnp.exp(final_cumulative_forgetting[None] - running_total)
    causal = causal_mask(query_block.shape[0])[None]
    similarity_weights = jnp.einsum('thk,shk->hts', probe_vector_scaled, key_rescaled, precision=exact_arithmetic_mode)
    similarity_weights = jnp.where(causal, similarity_weights, 0.0)
    pair_products = jnp.einsum('thv,shv->hts', result_derivative_piece, value_tile, precision=exact_arithmetic_mode)
    pair_products = jnp.where(causal, pair_products, 0.0)
    query_gradient = jnp.exp(running_total) * (jnp.einsum('ulm,muf->luf', pair_products, key_rescaled, precision=exact_arithmetic_mode) + jnp.einsum('lxp,xup->lxu', result_derivative_piece, initial_state, precision=exact_arithmetic_mode))
    key_gradient = jnp.exp(-running_total) * jnp.einsum('dxb,xdc->bdc', pair_products, probe_vector_scaled, precision=exact_arithmetic_mode) + jnp.exp(final_cumulative_forgetting[None] - running_total) * jnp.einsum('zod,qzd->qzo', incoming_memory, value_tile, precision=exact_arithmetic_mode)
    content_derivative = jnp.einsum('iay,aiz->yiz', similarity_weights, result_derivative_piece, precision=exact_arithmetic_mode) + jnp.einsum('oxa,rox->roa', incoming_memory, lookup_vector_leftover, precision=exact_arithmetic_mode)
    revised_memory = jnp.exp(final_cumulative_forgetting)[:, :, None] * incoming_memory + jnp.einsum('ygw,ygq->gwq', probe_vector_scaled, result_derivative_piece, precision=exact_arithmetic_mode)
    return (revised_memory, (query_gradient, key_gradient, content_derivative))

def section_grads(pieces):
    queries, forget_logits, values, gates, output_grad, lower_bound, norm_gain = pieces
    query_rows = queries.astype(jnp.float32)
    squashed = jax.nn.sigmoid(forget_logits.astype(jnp.float32))
    forget = lower_bound[None] + (1.0 - lower_bound[None]) * squashed
    key_rows = 1.0 - forget
    log_forget = jnp.log(forget)

    def split_blocks(matrix):
        return matrix.reshape(SEQUENCE_LENGTH // BLOCK, BLOCK, HEADS, DK)
    query_blocks = split_blocks(query_rows)
    key_blocks = split_blocks(key_rows)
    value_blocks = split_blocks(values.astype(jnp.float32))
    forget_blocks = split_blocks(log_forget)
    zero_state = jnp.zeros((HEADS, DK, DK), jnp.float32)
    final_state, (attended_blocks, start_states) = lax.scan(block_forward, zero_state, (query_blocks, key_blocks, value_blocks, forget_blocks))
    attended = attended_blocks.reshape(SEQUENCE_LENGTH, HEAD_COLUMNS)
    gate_rows = gates.astype(jnp.float32)
    grad_rows = output_grad.astype(jnp.float32)
    norm_grad = grad_rows * jax.nn.silu(gate_rows)
    squares = lax.optimization_barrier(jnp.sum(attended * attended, axis=1))
    weighted = lax.optimization_barrier(jnp.sum(norm_gain[None] * norm_grad * attended, axis=1))
    root = jnp.sqrt(squares / HEAD_COLUMNS + epsilon)[:, None]
    normed = attended / root * norm_gain[None]
    gated = jax.nn.sigmoid(gate_rows)
    gate_grad = grad_rows * normed * gated * (1.0 + gate_rows * (1.0 - gated))
    attended_grad = norm_gain[None] * norm_grad / root - attended * weighted[:, None] / (HEAD_COLUMNS * root ** 3)
    final_grad, (query_parts, key_parts, value_parts) = lax.scan(block_backward, zero_state, (query_blocks, key_blocks, value_blocks, forget_blocks, split_blocks(attended_grad), start_states), reverse=True)
    query_gradient = query_parts.reshape(SEQUENCE_LENGTH, HEAD_COLUMNS)
    key_gradient = key_parts.reshape(SEQUENCE_LENGTH, HEAD_COLUMNS)
    content_derivative = value_parts.reshape(SEQUENCE_LENGTH, HEAD_COLUMNS)
    base_terms = query_rows * query_gradient - key_rows * key_gradient
    log_grad = jnp.cumsum(base_terms[::-1], axis=0)[::-1]
    logit_grad = (log_grad / forget - key_gradient) * (1.0 - lower_bound[None]) * squashed * (1.0 - squashed)
    return (query_gradient.astype(jnp.bfloat16), logit_grad.astype(jnp.bfloat16), content_derivative.astype(jnp.bfloat16), gate_grad.astype(jnp.bfloat16))

def reference(queries, forget_logits, values, gates, output_grad, lower_bound, norm_gain):
    query_out, logit_out, value_out, gate_out = lax.map(section_grads, (queries, forget_logits, values, gates, output_grad, lower_bound, norm_gain))
    return (jnp.roll(query_out, -1, axis=0), jnp.roll(logit_out, -1, axis=0), jnp.roll(value_out, -1, axis=0), jnp.roll(gate_out, -1, axis=0))
```

```python
import functools

import jax
import jax.numpy as jnp
from jax import lax
from jax.experimental import pallas as pl
from jax.experimental.pallas import tpu as pltpu
from jax.sharding import PartitionSpec as P

DK = 128
BLOCK = 128
HEAD_COLUMNS = 4096
EPSILON = 1e-06

F32 = jnp.float32
BF16 = jnp.bfloat16
NN = ((1,), (0,))
NT = ((1,), (1,))
TN = ((0,), (0,))
PARAMS = pltpu.CompilerParams(vmem_limit_bytes=48 * 1024 * 1024)
VMEM = pl.BlockSpec(memory_space=pltpu.VMEM)


def parts(x, count=2):
    if x.dtype == BF16:
        return [x]
    terms = []
    for _ in range(count - 1):
        term = x.astype(BF16)
        terms.append(term)
        x = x - term.astype(F32)
    return terms + [x.astype(BF16)]


def product(left, right, dims):
    pairs = [
        (a, b)
        for i, a in enumerate(left)
        for j, b in enumerate(right)
        if i + j < max(len(left), len(right))
    ]
    lhs = jnp.concatenate([a for a, _ in pairs], axis=dims[0][0])
    rhs = jnp.concatenate([b for _, b in pairs], axis=dims[1][0])
    return lax.dot_general(lhs, rhs, (dims, ((), ())), preferred_element_type=F32)


def triangle(lower):
    row = lax.broadcasted_iota(jnp.int32, (BLOCK, BLOCK), 0)
    col = lax.broadcasted_iota(jnp.int32, (BLOCK, BLOCK), 1)
    return row >= col if lower else row <= col


def head_row(ref):
    start = pl.multiple_of(lax.axis_index("ctx") * DK, DK)
    return ref[0:1, pl.ds(start, DK)]


def gates_of(x, bound):
    squashed = jax.nn.sigmoid(x.astype(F32))
    forget = bound + (1.0 - bound) * squashed
    return squashed, forget


def pack_kernel(heads, *refs):
    out = refs[-1]
    for a, ref in enumerate(refs[:-1]):
        for h in range(heads):
            out[h, a] = ref[0, :, h * DK : (h + 1) * DK]


def pack(arrays):
    rows, width = arrays[0].shape[1:]
    steps = 4
    heads = width // DK
    each = heads // steps
    return pl.pallas_call(
        functools.partial(pack_kernel, each),
        grid=(steps,),
        out_shape=jax.ShapeDtypeStruct((heads, len(arrays), rows, DK), BF16),
        in_specs=[pl.BlockSpec((1, rows, each * DK), lambda i: (0, 0, i))] * len(arrays),
        out_specs=pl.BlockSpec((each, len(arrays), rows, DK), lambda i: (i, 0, 0, 0)),
        compiler_params=PARAMS,
        name="pack",
    )(*arrays)


def unpack_kernel(heads, ref, *outs):
    for a, out in enumerate(outs):
        for h in range(heads):
            out[0, :, h * DK : (h + 1) * DK] = ref[h, a]


def unpack(array):
    heads, count, rows, _ = array.shape
    steps = 4
    each = heads // steps
    return pl.pallas_call(
        functools.partial(unpack_kernel, each),
        grid=(steps,),
        out_shape=[jax.ShapeDtypeStruct((1, rows, heads * DK), BF16)] * count,
        in_specs=[pl.BlockSpec((each, count, rows, DK), lambda i: (i, 0, 0, 0))],
        out_specs=[pl.BlockSpec((1, rows, each * DK), lambda i: (0, 0, i))] * count,
        compiler_params=PARAMS,
        name="unpack",
    )(array)


def forward_kernel(x_ref, bound_ref, gain_ref, att_ref, state_ref, run_ref, score_ref, sums_ref, rows_ref):
    blocks = x_ref.shape[0]
    bound = head_row(bound_ref)
    gain = head_row(gain_ref)
    lower = triangle(True)
    ones_below = [jnp.where(lower, 1.0, 0.0).astype(BF16)]
    ones = [jnp.ones((8, DK), BF16)]

    def turn(b, state):
        q = x_ref[b, 0].astype(F32)
        v = x_ref[b, 2]
        squashed, forget = gates_of(x_ref[b, 1], bound)
        keys = 1.0 - forget
        run = product(ones_below, parts(jnp.log(forget), 3), NN)
        last = run[BLOCK - 1 : BLOCK]
        q_scaled = parts(q * jnp.exp(run))
        k_scaled = parts(keys * jnp.exp(-run))
        k_left = parts(keys * jnp.exp(last - run))
        scores = jnp.where(lower, product(q_scaled, k_scaled, NT), 0.0)
        attended = product(parts(scores), [v], NN) + product(q_scaled, parts(state), NT)
        att_ref[b] = attended
        state_ref[b] = state
        run_ref[b] = run
        score_ref[b] = scores
        gates = x_ref[b, 3].astype(F32)
        norm_grad = x_ref[b, 4].astype(F32) * (gates * jax.nn.sigmoid(gates))
        rows_ref[b] = product(ones, parts(attended * attended, 3), NT)
        rows_ref[b + blocks] = product(ones, parts(gain * norm_grad * attended, 3), NT)
        return state * jnp.exp(last) + product([v], k_left, TN)

    lax.fori_loop(0, blocks, turn, jnp.zeros((DK, DK), F32), unroll=2)
    rows = jnp.concatenate([rows_ref[i, 0:1] for i in range(2 * blocks)], axis=0)
    for i in range(blocks):
        sums_ref[i] = rows


def forward(x, bound, gain):
    blocks = x.shape[0]
    square = jax.ShapeDtypeStruct((blocks, BLOCK, DK), F32)
    return pl.pallas_call(
        forward_kernel,
        out_shape=[square, square, square, square, jax.ShapeDtypeStruct((blocks, 2 * blocks, BLOCK), F32)],
        in_specs=[VMEM] * 3,
        out_specs=[VMEM] * 5,
        scratch_shapes=[pltpu.VMEM((2 * blocks, 8, BLOCK), F32)],
        compiler_params=PARAMS,
        name="forward",
    )(x, bound, gain)


def backward_kernel(
    x_ref, bound_ref, gain_ref, att_ref, state_ref, run_ref, score_ref, mine_ref, other_ref,
    gq_ref, vl_ref, root_ref, pull_ref,
):
    blocks = x_ref.shape[0]
    bound = head_row(bound_ref)
    gain = head_row(gain_ref)
    lower = triangle(True)
    ones_above = [jnp.where(triangle(False), 1.0, 0.0).astype(BF16)]

    sums = mine_ref[0] + other_ref[0]
    for i in range(1, blocks):
        sums = sums + (mine_ref[i] + other_ref[i])
    root = jnp.sqrt(sums[:blocks] / HEAD_COLUMNS + EPSILON)
    inverse = 1.0 / root
    pull = sums[blocks:] / (HEAD_COLUMNS * (root * root * root))
    fill = jnp.zeros((BLOCK - 2 * blocks, BLOCK), F32)
    columns = jnp.concatenate([inverse, pull, fill], axis=0).T
    for i in range(blocks):
        root_ref[i] = jnp.broadcast_to(columns[:, i : i + 1], (BLOCK, DK))
        pull_ref[i] = jnp.broadcast_to(columns[:, blocks + i : blocks + i + 1], (BLOCK, DK))

    def turn(step, carried):
        later, log_later = carried
        b = blocks - 1 - step
        q = x_ref[b, 0].astype(F32)
        v = x_ref[b, 2]
        squashed, forget = gates_of(x_ref[b, 1], bound)
        keys = 1.0 - forget
        gates = x_ref[b, 3].astype(F32)
        grad = x_ref[b, 4].astype(F32)
        gated = jax.nn.sigmoid(gates)
        attended = att_ref[b]
        over_root = root_ref[b]
        normed = attended * over_root * gain
        gq_ref[b, 0] = (grad * normed * gated * (1.0 + gates * (1.0 - gated))).astype(BF16)
        dout = gain * (grad * (gates * gated)) * over_root - attended * pull_ref[b]

        run = run_ref[b]
        last = run[BLOCK - 1 : BLOCK]
        grow = jnp.exp(run)
        shrink = jnp.exp(-run)
        left = jnp.exp(last - run)
        q_scaled = parts(q * grow)
        k_scaled = parts(keys * shrink)
        k_left = parts(keys * left)
        douts = parts(dout)
        laters = parts(later)
        pairs = parts(jnp.where(lower, product(douts, [v], NT), 0.0))
        q_grad = grow * (product(pairs, k_scaled, NN) + product(douts, parts(state_ref[b]), NN))
        k_grad = shrink * product(pairs, q_scaled, TN) + left * product([v], laters, NN)
        v_grad = product(parts(score_ref[b]), douts, TN) + product(k_left, laters, NT)
        terms = q * q_grad - keys * k_grad
        log_grad = product(ones_above, parts(terms, 3), NN) + log_later
        logit_grad = (log_grad / forget - k_grad) * (1.0 - bound) * squashed * (1.0 - squashed)
        gq_ref[b, 1] = q_grad.astype(BF16)
        vl_ref[b, 0] = v_grad.astype(BF16)
        vl_ref[b, 1] = logit_grad.astype(BF16)
        later = later * jnp.exp(last) + product(douts, q_scaled, TN)
        return later, jnp.sum(state_ref[b] * later, axis=0, keepdims=True)

    lax.fori_loop(
        0, blocks, turn, (jnp.zeros((DK, DK), F32), jnp.zeros((1, DK), F32)), unroll=2
    )


def backward(x, bound, gain, attended, states, runs, scores, mine, other):
    blocks = x.shape[0]
    pair = jax.ShapeDtypeStruct((blocks, 2, BLOCK, DK), BF16)
    return pl.pallas_call(
        backward_kernel,
        out_shape=[pair, pair],
        in_specs=[VMEM] * 9,
        out_specs=[VMEM] * 2,
        scratch_shapes=[pltpu.VMEM((blocks, BLOCK, DK), F32)] * 2,
        compiler_params=PARAMS,
        name="backward",
    )(x, bound, gain, attended, states, runs, scores, mine, other)


def to_previous_section(x):
    size = lax.axis_size("pipe")
    return lax.ppermute(x, "pipe", [(i, (i - 1) % size) for i in range(size)])


def exchange(x):
    return lax.all_to_all(x, "ctx", 0, 0)


def body(queries, forget_logits, values, gates, output_grad, lower_bound, norm_gain):
    x = exchange(pack([queries, forget_logits, values, gates, output_grad]))
    attended, states, runs, scores, sums = forward(x, lower_bound, norm_gain)
    mine = exchange(sums)
    other = lax.ppermute(mine, "tp", [(0, 1), (1, 0)])
    gq, vl = backward(x, lower_bound, norm_gain, attended, states, runs, scores, mine, other)
    gq_there = to_previous_section(gq)
    vl_back = exchange(vl)
    vl_there = to_previous_section(vl_back)
    gate_grad, query_grad = unpack(exchange(gq_there))
    value_grad, logit_grad = unpack(vl_there)
    return query_grad, logit_grad, value_grad, gate_grad


def solution(mesh):
    rows = P("pipe", "ctx", "tp")
    return jax.shard_map(
        body,
        mesh=mesh,
        in_specs=(rows,) * 5 + (P("pipe", "tp"),) * 2,
        out_specs=(rows,) * 4,
        check_vma=False,
    )
```

```python
import functools

import jax
import jax.numpy as jnp
from jax import lax
from jax.experimental import pallas as pl
from jax.experimental.pallas import tpu as pltpu
from jax.sharding import PartitionSpec as P

DK = 128
BLOCK = 128
HEAD_COLUMNS = 4096
EPSILON = 1e-06

F32 = jnp.float32
BF16 = jnp.bfloat16
NN = ((1,), (0,))
NT = ((1,), (1,))
TN = ((0,), (0,))
UNROLL = 4
PARAMS = pltpu.CompilerParams(vmem_limit_bytes=24 * 1024 * 1024)
VMEM = pl.BlockSpec(memory_space=pltpu.VMEM)


def parts(x, count=2):
    if x.dtype == BF16:
        return [x]
    terms = []
    for _ in range(count - 1):
        term = x.astype(BF16)
        terms.append(term)
        x = x - term.astype(F32)
    return terms + [x.astype(BF16)]


def product(left, right, dims):
    pairs = [
        (a, b)
        for i, a in enumerate(left)
        for j, b in enumerate(right)
        if i + j < max(len(left), len(right))
    ]
    lhs = jnp.concatenate([a for a, _ in pairs], axis=dims[0][0])
    rhs = jnp.concatenate([b for _, b in pairs], axis=dims[1][0])
    return lax.dot_general(lhs, rhs, (dims, ((), ())), preferred_element_type=F32)


def triangle(lower):
    row = lax.broadcasted_iota(jnp.int32, (BLOCK, BLOCK), 0)
    col = lax.broadcasted_iota(jnp.int32, (BLOCK, BLOCK), 1)
    return row >= col if lower else row <= col


def head_row(ref):
    start = pl.multiple_of(lax.axis_index("ctx") * DK, DK)
    return ref[0:1, pl.ds(start, DK)]


def pack_kernel(*refs):
    *arrays, out, landed, sems = refs
    copies = [pltpu.make_async_copy(ref, landed.at[a], sems.at[a]) for a, ref in enumerate(arrays)]
    for copy in copies:
        copy.start()
    for a, copy in enumerate(copies):
        copy.wait()
        for h in range(out.shape[0]):
            out[h, a] = landed[a, 0, :, h * DK : (h + 1) * DK]


def pack(arrays):
    count = len(arrays)
    rows, width = arrays[0].shape[1:]
    return pl.pallas_call(
        pack_kernel,
        out_shape=jax.ShapeDtypeStruct((width // DK, count, rows, DK), BF16),
        in_specs=[pl.BlockSpec(memory_space=pl.ANY)] * count,
        out_specs=VMEM,
        scratch_shapes=[pltpu.VMEM((count, 1, rows, width), BF16), pltpu.SemaphoreType.DMA((count,))],
        compiler_params=pltpu.CompilerParams(vmem_limit_bytes=58 * 1024 * 1024),
        name="pack",
    )(*arrays)


def unpack_kernel(heads, ref, *outs):
    for a, out in enumerate(outs):
        for h in range(heads):
            out[0, :, h * DK : (h + 1) * DK] = ref[h, a]


def unpack(array):
    heads, count, rows, _ = array.shape
    steps = 4
    each = heads // steps
    return pl.pallas_call(
        functools.partial(unpack_kernel, each),
        grid=(steps,),
        out_shape=[jax.ShapeDtypeStruct((1, rows, heads * DK), BF16)] * count,
        in_specs=[pl.BlockSpec((each, count, rows, DK), lambda i: (i, 0, 0, 0))],
        out_specs=[pl.BlockSpec((1, rows, each * DK), lambda i: (0, 0, i))] * count,
        compiler_params=PARAMS,
        name="unpack",
    )(array)


def forward_kernel(
    x_ref, bound_ref, gain_ref,
    att_ref, pull_ref, gate_ref, squash_ref, grow_ref, shrink_ref, q_ref, k_ref, state_ref, score_ref, sums_ref,
):
    blocks = x_ref.shape[0]
    bound = head_row(bound_ref)
    gain = head_row(gain_ref)
    lower = triangle(True)
    ones_below = [jnp.where(lower, 1.0, 0.0).astype(BF16)]
    lane = lax.broadcasted_iota(jnp.int32, (BLOCK, DK), 1)

    def turn(b, carried):
        state, columns = carried
        q = x_ref[b, 0].astype(F32)
        v = x_ref[b, 2]
        squashed = jax.nn.sigmoid(x_ref[b, 1].astype(F32))
        forget = bound + (1.0 - bound) * squashed
        run = product(ones_below, parts(jnp.log(forget), 3), NN)
        grow = jnp.exp(run)
        shrink = jnp.exp(-run)
        q_scaled = parts(q * grow)
        k_scaled = parts((1.0 - forget) * shrink)
        states = parts(state)
        scores = parts(jnp.where(lower, product(q_scaled, k_scaled, NT), 0.0))
        attended = product(scores, [v], NN) + product(q_scaled, states, NT)
        gates = x_ref[b, 3].astype(F32)
        gated = jax.nn.sigmoid(gates)
        grad = x_ref[b, 4].astype(F32) * gain
        pull = grad * (gates * gated)
        att_ref[b] = attended
        pull_ref[b] = pull
        gate_ref[b] = grad * gated * (1.0 + gates * (1.0 - gated))
        squash_ref[b] = squashed
        grow_ref[b] = grow
        shrink_ref[b] = shrink
        for ref, terms in ((q_ref, q_scaled), (k_ref, k_scaled), (state_ref, states), (score_ref, scores)):
            ref[b, 0], ref[b, 1] = terms
        square = jnp.sum(attended * attended, axis=1, keepdims=True)
        weighted = jnp.sum(pull * attended, axis=1, keepdims=True)
        columns = jnp.where(lane == b, square, jnp.where(lane == b + blocks, weighted, columns))
        return (state + product([v], k_scaled, TN)) * grow[BLOCK - 1 : BLOCK], columns

    nothing = jnp.zeros((BLOCK, DK), F32)
    _, columns = lax.fori_loop(0, blocks, turn, (nothing, nothing), unroll=UNROLL)
    rows = columns.T[: 2 * blocks]
    for i in range(blocks):
        sums_ref[i] = rows


def forward(x, bound, gain):
    blocks = x.shape[0]
    square = jax.ShapeDtypeStruct((blocks, BLOCK, DK), F32)
    pair = jax.ShapeDtypeStruct((blocks, 2, BLOCK, DK), BF16)
    sums = jax.ShapeDtypeStruct((blocks, 2 * blocks, BLOCK), F32)
    return pl.pallas_call(
        forward_kernel,
        out_shape=[square] * 6 + [pair] * 4 + [sums],
        in_specs=[VMEM] * 3,
        out_specs=[VMEM] * 11,
        compiler_params=PARAMS,
        name="forward",
    )(x, bound, gain)


def backward_kernel(
    x_ref, bound_ref, gain_ref,
    att_ref, pull_ref, gate_ref, squash_ref, grow_ref, shrink_ref, q_ref, k_ref, state_ref, score_ref,
    mine_ref, other_ref,
    gq_ref, vl_ref, root_ref, weigh_ref,
):
    blocks = x_ref.shape[0]
    bound = head_row(bound_ref)
    lower = triangle(True)
    ones_above = [jnp.where(triangle(False), 1.0, 0.0).astype(BF16)]

    sums = mine_ref[0] + other_ref[0]
    for i in range(1, blocks):
        sums = sums + (mine_ref[i] + other_ref[i])
    root = jnp.sqrt(sums[:blocks] / HEAD_COLUMNS + EPSILON)
    inverse = 1.0 / root
    weigh = sums[blocks:] / (HEAD_COLUMNS * (root * root * root))
    fill = jnp.zeros((BLOCK - 2 * blocks, BLOCK), F32)
    columns = jnp.concatenate([inverse, weigh, fill], axis=0).T
    for i in range(blocks):
        root_ref[i] = jnp.broadcast_to(columns[:, i : i + 1], (BLOCK, DK))
        weigh_ref[i] = jnp.broadcast_to(columns[:, blocks + i : blocks + i + 1], (BLOCK, DK))

    def turn(step, carried):
        later, log_later = carried
        b = blocks - 1 - step
        q = x_ref[b, 0].astype(F32)
        v = x_ref[b, 2]
        squashed = squash_ref[b]
        forget = bound + (1.0 - bound) * squashed
        attended = att_ref[b]
        over_root = root_ref[b]
        gq_ref[b, 0] = (gate_ref[b] * (attended * over_root)).astype(BF16)
        douts = parts(pull_ref[b] * over_root - attended * weigh_ref[b])

        grow = grow_ref[b]
        q_scaled = [q_ref[b, 0], q_ref[b, 1]]
        k_scaled = [k_ref[b, 0], k_ref[b, 1]]
        states = [state_ref[b, 0], state_ref[b, 1]]
        scores = [score_ref[b, 0], score_ref[b, 1]]
        later = later * grow[BLOCK - 1 : BLOCK]
        laters = parts(later)
        pairs = parts(jnp.where(lower, product(douts, [v], NT), 0.0))
        q_grad = grow * (product(pairs, k_scaled, NN) + product(douts, states, NN))
        k_grad = shrink_ref[b] * (product(pairs, q_scaled, TN) + product([v], laters, NN))
        v_grad = product(scores, douts, TN) + product(k_scaled, laters, NT)
        terms = q * q_grad - (1.0 - forget) * k_grad
        log_grad = product(ones_above, parts(terms, 3), NN) + log_later
        logit_grad = (log_grad / forget - k_grad) * (1.0 - bound) * squashed * (1.0 - squashed)
        gq_ref[b, 1] = q_grad.astype(BF16)
        vl_ref[b, 0] = v_grad.astype(BF16)
        vl_ref[b, 1] = logit_grad.astype(BF16)
        later = later + product(douts, q_scaled, TN)
        state = states[0].astype(F32) + states[1].astype(F32)
        return later, jnp.sum(state * later, axis=0, keepdims=True)

    lax.fori_loop(
        0, blocks, turn, (jnp.zeros((DK, DK), F32), jnp.zeros((1, DK), F32)), unroll=UNROLL
    )


def backward(x, bound, gain, *saved):
    blocks = x.shape[0]
    pair = jax.ShapeDtypeStruct((blocks, 2, BLOCK, DK), BF16)
    return pl.pallas_call(
        backward_kernel,
        out_shape=[pair, pair],
        in_specs=[VMEM] * (3 + len(saved)),
        out_specs=[VMEM] * 2,
        scratch_shapes=[pltpu.VMEM((blocks, BLOCK, DK), F32)] * 2,
        compiler_params=PARAMS,
        name="backward",
    )(x, bound, gain, *saved)


def to_previous_section(x):
    size = lax.axis_size("pipe")
    return lax.ppermute(x, "pipe", [(i, (i - 1) % size) for i in range(size)])


def exchange(x):
    return lax.all_to_all(x, "ctx", 0, 0)


def body(queries, forget_logits, values, gates, output_grad, lower_bound, norm_gain):
    x = exchange(pack([queries, forget_logits, values, gates, output_grad]))
    *saved, sums = forward(x, lower_bound, norm_gain)
    mine = exchange(sums)
    other = lax.ppermute(mine, "tp", [(0, 1), (1, 0)])
    gq, vl = backward(x, lower_bound, norm_gain, *saved, mine, other)
    gq_there = to_previous_section(gq)
    vl_there = to_previous_section(exchange(vl))
    gate_grad, query_grad = unpack(exchange(gq_there))
    value_grad, logit_grad = unpack(vl_there)
    return query_grad, logit_grad, value_grad, gate_grad


def solution(mesh):
    rows = P("pipe", "ctx", "tp")
    return jax.shard_map(
        body,
        mesh=mesh,
        in_specs=(rows,) * 5 + (P("pipe", "tp"),) * 2,
        out_specs=(rows,) * 4,
        check_vma=False,
    )
```

```python
import functools

import jax
import jax.numpy as jnp
from jax import lax
from jax.experimental import pallas as pl
from jax.experimental.pallas import tpu as pltpu
from jax.sharding import PartitionSpec as P

DK = 128
BLOCK = 128
HEAD_COLUMNS = 4096
EPSILON = 1e-06

F32 = jnp.float32
BF16 = jnp.bfloat16
NN = ((1,), (0,))
NT = ((1,), (1,))
TN = ((0,), (0,))
RANGE = 84.0
EXTRA = 16
PIECES = 4
PARAMS = pltpu.CompilerParams(vmem_limit_bytes=24 * 1024 * 1024)
VMEM = pl.BlockSpec(memory_space=pltpu.VMEM)


def parts(x, count=2):
    if x.dtype == BF16:
        return [x]
    terms = []
    for _ in range(count - 1):
        term = x.astype(BF16)
        terms.append(term)
        x = x - term.astype(F32)
    return terms + [x.astype(BF16)]


def product(left, right, dims):
    pairs = [
        (a, b)
        for i, a in enumerate(left)
        for j, b in enumerate(right)
        if i + j < max(len(left), len(right))
    ]
    lhs = jnp.concatenate([a for a, _ in pairs], axis=dims[0][0])
    rhs = jnp.concatenate([b for _, b in pairs], axis=dims[1][0])
    return lax.dot_general(lhs, rhs, (dims, ((), ())), preferred_element_type=F32)


def triangle(lower):
    row = lax.broadcasted_iota(jnp.int32, (BLOCK, BLOCK), 0)
    col = lax.broadcasted_iota(jnp.int32, (BLOCK, BLOCK), 1)
    return row >= col if lower else row <= col


def of_head(ref, h):
    return ref[0, :, pl.ds(pl.multiple_of(h * DK, DK), DK)]


def row_of_head(ref, h):
    return ref[0:1, pl.ds(pl.multiple_of(h * DK, DK), DK)]


def put_head(ref, h, value):
    ref[0, :BLOCK, pl.ds(pl.multiple_of(h * DK, DK), DK)] = value


def pair_of(ref, h):
    return [ref[h, 0], ref[h, 1]]


def put_pair(ref, h, terms):
    ref[h, 0], ref[h, 1] = terms


def sum_of(terms):
    return terms[0].astype(F32) + terms[1].astype(F32)


def forget_of(squashed, bound):
    return bound + (1.0 - bound) * squashed


def encode(ref, i, x, *rows):
    top = jnp.maximum(jnp.max(jnp.abs(x), axis=0, keepdims=True), 1e-30)
    top = (top * 1.01).astype(BF16).astype(F32)
    ref[i, :DK] = jnp.exp(x * (RANGE / top)).astype(BF16)
    place = lax.broadcasted_iota(jnp.int32, (EXTRA, DK), 0)
    extra = jnp.zeros((EXTRA, DK), F32)
    for r, row in enumerate((top,) + rows):
        extra = jnp.where(place == r, row, extra)
    ref[i, DK:] = extra.astype(BF16)


def decode(ref, i):
    extra = ref[i, DK:].astype(F32)
    return jnp.log(ref[i, :DK].astype(F32)) * (extra[0:1] * (1.0 / RANGE)), extra


def call(kernel, name, ins, outs, streamed=(), kept=(), scratch=()):
    hbm = pl.BlockSpec(memory_space=pltpu.HBM)
    return pl.pallas_call(
        kernel,
        out_shape=[*outs, *kept],
        in_specs=[hbm] * len(streamed) + [VMEM] * len(ins),
        out_specs=[VMEM] * len(outs) + [hbm] * len(kept),
        scratch_shapes=scratch,
        compiler_params=PARAMS,
        name=name,
    )(*[pltpu.with_memory_space_constraint(x, pltpu.HBM) for x in streamed], *ins)


def buffers(*arrays):
    return [pltpu.VMEM(x.shape, x.dtype) for x in arrays] + [pltpu.SemaphoreType.DMA((len(arrays), PIECES))]


def piece_of(ref, p):
    if ref.shape[0] == 1:
        width = ref.shape[2] // PIECES
        return ref.at[:, :, pl.ds(p * width, width)]
    each = ref.shape[0] // PIECES
    return ref.at[pl.ds(p * each, each)]


def start_piece(sources, targets, sems, p):
    copies = [
        pltpu.make_async_copy(piece_of(source, p), piece_of(target, p), sems.at[a, p])
        for a, (source, target) in enumerate(zip(sources, targets))
    ]
    for copy in copies:
        copy.start()
    return copies


def start_copies(sources, targets, sems, heads):
    copies = [start_piece(sources, targets, sems, p) for p in range(PIECES)]

    def wait(h):
        if h % (heads // PIECES) == 0:
            for copy in copies[h * PIECES // heads]:
                copy.wait()

    return wait


def own_state_kernel(
    logit_hbm, value_hbm, bound_ref, run_ref, k_ref, own_ref, v_ref, coded_ref,
    logit_ref, value_ref, sems,
):
    wait = start_copies((logit_hbm, value_hbm), (logit_ref, value_ref), sems, own_ref.shape[0])
    ones_below = [jnp.where(triangle(True), 1.0, 0.0).astype(BF16)]
    for h in range(own_ref.shape[0]):
        wait(h)
        bound = row_of_head(bound_ref, h)
        squashed = jax.nn.sigmoid(of_head(logit_ref, h).astype(F32))
        forget = forget_of(squashed, bound)
        run = product(ones_below, parts(jnp.log(forget), 3), NN)
        k_scaled = parts((1.0 - forget) * jnp.exp(-run))
        last = run[BLOCK - 1 : BLOCK]
        v = of_head(value_ref, h)
        own = product([v], k_scaled, TN) * jnp.exp(last)
        run_ref[h] = run
        v_ref[h] = v
        put_pair(k_ref, h, k_scaled)
        own_ref[h] = own
        encode(coded_ref, h, own, *[term.astype(F32) for term in parts(last, 3)])


def states_before_kernel(coded_ref, out_ref, decay_ref):
    state = jnp.zeros((DK, DK), F32)
    for i in range(coded_ref.shape[0]):
        encode(out_ref, i, state)
        own, extra = decode(coded_ref, i)
        decay = jnp.exp(extra[1:2] + extra[2:3] + extra[3:4])
        decay_ref[i] = jnp.broadcast_to(decay, decay_ref.shape[1:])
        state = state * decay + own


def states_after_kernel(coded_ref, decay_ref, out_ref):
    later = jnp.zeros((DK, DK), F32)
    for i in reversed(range(coded_ref.shape[0])):
        encode(out_ref, i, later)
        later = later * decay_ref[i, 0:1] + decode(coded_ref, i)[0]


def attended_kernel(
    query_hbm, gates_hbm, grad_hbm, coded_ref, gain_ref, run_ref, k_ref, v_ref,
    q_ref, grow_ref, score_ref, pull_ref, gate_ref, att_ref, state_ref, sums_ref,
    query_ref, gates_ref, grad_ref, sems,
):
    wait = start_copies((query_hbm, gates_hbm, grad_hbm), (query_ref, gates_ref, grad_ref), sems, v_ref.shape[0])
    lower = triangle(True)
    squares = jnp.zeros((BLOCK, DK), F32)
    weighted = squares
    for h in range(v_ref.shape[0]):
        wait(h)
        grow = jnp.exp(run_ref[h])
        q_scaled = parts(of_head(query_ref, h).astype(F32) * grow)
        scores = parts(jnp.where(lower, product(q_scaled, pair_of(k_ref, h), NT), 0.0))
        states = parts(decode(coded_ref, h)[0])
        attended = product(scores, [v_ref[h]], NN) + product(q_scaled, states, NT)
        gates = of_head(gates_ref, h).astype(F32)
        gated = jax.nn.sigmoid(gates)
        grad = of_head(grad_ref, h).astype(F32) * row_of_head(gain_ref, h)
        pull = grad * (gates * gated)
        put_pair(q_ref, h, q_scaled)
        grow_ref[h] = grow
        put_pair(score_ref, h, scores)
        pull_ref[h] = pull
        gate_ref[h] = grad * gated * (1.0 + gates * (1.0 - gated))
        att_ref[h] = attended
        put_pair(state_ref, h, states)
        squares = squares + attended * attended
        weighted = weighted + pull * attended
    for i, total in enumerate((squares, weighted)):
        sums_ref[8 * i : 8 * i + 8] = jnp.broadcast_to(jnp.sum(total.T, axis=0, keepdims=True), (8, BLOCK))


def early_grads_kernel(
    mine_ref, other_ref, att_ref, pull_ref, gate_ref, grow_ref, q_ref, k_ref, v_ref, own_ref, state_ref, score_ref,
    coded_ref, gate_grad_ref, query_grad_ref, kept_hbm, kept_ref, sems,
):
    heads = v_ref.shape[0]
    copies = []
    ones_above = [jnp.where(triangle(False), 1.0, 0.0).astype(BF16)]
    sums = mine_ref[...] + other_ref[...]
    root = jnp.sqrt(sums[0:8] / HEAD_COLUMNS + EPSILON)
    weigh = sums[8:16] / (HEAD_COLUMNS * (root * root * root))
    fill = jnp.zeros((BLOCK - 16, BLOCK), F32)
    columns = jnp.concatenate([1.0 / root, weigh, fill], axis=0).T
    over_root = jnp.broadcast_to(columns[:, 0:1], (BLOCK, DK))
    weigh = jnp.broadcast_to(columns[:, 8:9], (BLOCK, DK))
    lower = triangle(True)
    for h in range(v_ref.shape[0]):
        attended = att_ref[h]
        put_head(gate_grad_ref, h, (gate_ref[h] * (attended * over_root)).astype(BF16))
        douts = parts(pull_ref[h] * over_root - attended * weigh)
        q_scaled = pair_of(q_ref, h)
        encode(coded_ref, h, product(douts, q_scaled, TN))
        pairs = parts(jnp.where(lower, product(douts, [v_ref[h]], NT), 0.0))
        k_scaled = pair_of(k_ref, h)
        states = pair_of(state_ref, h)
        q_part = product(pairs, k_scaled, NN) + product(douts, states, NN)
        k_part = product(pairs, q_scaled, TN)
        grow = grow_ref[h]
        put_head(query_grad_ref, h, (grow * q_part).astype(BF16))
        keys = sum_of(k_scaled)
        terms = sum_of(q_scaled) * q_part - keys * k_part
        shrink = 1.0 / grow
        kept_ref[h, 0] = product(ones_above, parts(terms, 3), NN) / (1.0 - keys * grow) - shrink * k_part
        kept_ref[h, 1] = product(pair_of(score_ref, h), douts, TN)
        kept_ref[h, 2] = shrink
        kept_ref[h, 3] = sum_of(states) * grow[BLOCK - 1 : BLOCK] + own_ref[h]
        if (h + 1) % (heads // PIECES) == 0:
            copies += start_piece((kept_ref,), (kept_hbm,), sems, h * PIECES // heads)
    for copy in copies:
        copy.wait()


def late_grads_kernel(
    logit_hbm, value_hbm, kept_hbm, coded_ref, bound_ref, value_grad_ref, logit_grad_ref,
    logit_ref, value_ref, kept_ref, sems,
):
    heads = kept_ref.shape[0]
    wait = start_copies((logit_hbm, value_hbm, kept_hbm), (logit_ref, value_ref, kept_ref), sems, heads)
    ones_above = [jnp.where(triangle(False), 1.0, 0.0).astype(BF16)]
    for h in range(heads):
        wait(h)
        later = decode(coded_ref, h)[0]
        shrink = kept_ref[h, 2]
        bound = row_of_head(bound_ref, h)
        squashed = jax.nn.sigmoid(of_head(logit_ref, h).astype(F32))
        forget = forget_of(squashed, bound)
        k_scaled = (1.0 - forget) * shrink
        log_later = jnp.sum(kept_ref[h, 3] * later, axis=0, keepdims=True)
        laters = parts(later / shrink[BLOCK - 1 : BLOCK])
        v_grad = kept_ref[h, 1] + product(parts(k_scaled), laters, NT)
        put_head(value_grad_ref, h, v_grad.astype(BF16))
        k_part = product([of_head(value_ref, h)], laters, NN)
        log_grad = log_later - product(ones_above, parts(k_scaled * k_part, 3), NN)
        logit_grad = kept_ref[h, 0] + (log_grad / forget - shrink * k_part)
        put_head(logit_grad_ref, h, (logit_grad * (1.0 - bound) * squashed * (1.0 - squashed)).astype(BF16))


def deliver_kernel(*refs):
    *refs, sems = refs
    half = len(refs) // 2
    copies = [
        pltpu.make_async_copy(source.at[:, :BLOCK], target, sems.at[a])
        for a, (source, target) in enumerate(zip(refs[:half], refs[half:]))
    ]
    for copy in copies:
        copy.start()
    for copy in copies:
        copy.wait()


def deliver(*arrays):
    hbm = pl.BlockSpec(memory_space=pltpu.HBM)
    return pl.pallas_call(
        deliver_kernel,
        out_shape=[jax.ShapeDtypeStruct((x.shape[0], BLOCK, x.shape[2]), x.dtype) for x in arrays],
        in_specs=[VMEM] * len(arrays),
        out_specs=[hbm] * len(arrays),
        scratch_shapes=[pltpu.SemaphoreType.DMA((len(arrays),))],
        compiler_params=pltpu.CompilerParams(vmem_limit_bytes=24 * 1024 * 1024),
        name="deliver",
    )(*arrays)


def to_previous_section(x):
    size = lax.axis_size("pipe")
    return lax.ppermute(x, "pipe", [(i, (i - 1) % size) for i in range(size)])


def exchange(x):
    return lax.all_to_all(x, "ctx", 0, 0)


def body(queries, forget_logits, values, gates, output_grad, lower_bound, norm_gain):
    heads = queries.shape[2] // DK
    whole = jax.ShapeDtypeStruct(queries.shape, BF16)
    square = jax.ShapeDtypeStruct((heads, BLOCK, DK), F32)
    pair = jax.ShapeDtypeStruct((heads, 2, BLOCK, DK), BF16)
    coded = jax.ShapeDtypeStruct((heads, DK + EXTRA, DK), BF16)
    decays = jax.ShapeDtypeStruct((heads, 8, DK), F32)
    sums = jax.ShapeDtypeStruct((16, BLOCK), F32)
    plain = jax.ShapeDtypeStruct((heads, BLOCK, DK), BF16)
    kept = jax.ShapeDtypeStruct((heads, 4, BLOCK, DK), F32)

    run, k_scaled, own_state, v, sent = call(
        own_state_kernel, "own_state", [lower_bound], [square, pair, square, plain, coded],
        streamed=[forget_logits, values], scratch=buffers(whole, whole),
    )
    sent, decay = call(states_before_kernel, "states_before", [exchange(sent)], [coded, decays])
    q_scaled, grow, scores, pull, gate_factor, attended, states, mine = call(
        attended_kernel, "attended", [exchange(sent), norm_gain, run, k_scaled, v],
        [pair, square, pair, square, square, square, pair, sums], streamed=[queries, gates, output_grad],
        scratch=buffers(whole, whole, whole),
    )
    other = lax.ppermute(mine, "tp", [(0, 1), (1, 0)])
    sent, gate_grad, query_grad, kept_now = call(
        early_grads_kernel, "early_grads",
        [mine, other, attended, pull, gate_factor, grow, q_scaled, k_scaled, v, own_state, states, scores],
        [coded, whole, whole], kept=[kept], scratch=buffers(kept),
    )
    gate_grad = to_previous_section(gate_grad)
    query_grad = to_previous_section(query_grad)

    def through(sent, decay):
        (sent,) = call(states_after_kernel, "states_after", [exchange(sent), decay], [coded])
        return exchange(sent)

    arrived = lax.cond(lower_bound[0, 0] > -1.0, through, lambda sent, decay: sent, sent, decay)
    arrived, gate_grad, query_grad = lax.optimization_barrier((arrived, gate_grad, query_grad))
    value_grad, logit_grad = call(
        late_grads_kernel, "late_grads", [arrived, lower_bound], [whole, whole],
        streamed=[forget_logits, values, kept_now], scratch=buffers(whole, whole, kept),
    )
    value_grad, logit_grad = to_previous_section(value_grad), to_previous_section(logit_grad)
    gate_grad, query_grad = deliver(gate_grad, query_grad)
    value_grad, logit_grad = deliver(value_grad, logit_grad)
    return query_grad, logit_grad, value_grad, gate_grad


def solution(mesh):
    rows = P("pipe", "ctx", "tp")
    return jax.shard_map(
        body,
        mesh=mesh,
        in_specs=(rows,) * 5 + (P("pipe", "tp"),) * 2,
        out_specs=(rows,) * 4,
        check_vma=False,
    )
```

```python
import functools

import jax
import jax.numpy as jnp
from jax import lax
from jax.experimental import pallas as pl
from jax.experimental.pallas import tpu as pltpu
from jax.sharding import PartitionSpec as P

DK = 128
BLOCK = 128
HEAD_COLUMNS = 4096
EPSILON = 1e-06

F32 = jnp.float32
BF16 = jnp.bfloat16
NN = ((1,), (0,))
NT = ((1,), (1,))
TN = ((0,), (0,))
RANGE = 84.0
EXTRA = 16
PIECES = 4
GROUP = 4
SHARES = (3, 4, 1)
PARAMS = pltpu.CompilerParams(vmem_limit_bytes=24 * 1024 * 1024)
VMEM = pl.BlockSpec(memory_space=pltpu.VMEM)
SMEM = pl.BlockSpec(memory_space=pltpu.SMEM)


def parts(x, count=2):
    if x.dtype == BF16:
        return [x]
    terms = []
    for _ in range(count - 1):
        term = x.astype(BF16)
        terms.append(term)
        x = x - term.astype(F32)
    return terms + [x.astype(BF16)]


def product(left, right, dims):
    pairs = [
        (a, b)
        for i, a in enumerate(left)
        for j, b in enumerate(right)
        if i + j < max(len(left), len(right))
    ]
    lhs = jnp.concatenate([a for a, _ in pairs], axis=dims[0][0])
    rhs = jnp.concatenate([b for _, b in pairs], axis=dims[1][0])
    return lax.dot_general(lhs, rhs, (dims, ((), ())), preferred_element_type=F32)


def triangle(lower):
    row = lax.broadcasted_iota(jnp.int32, (BLOCK, BLOCK), 0)
    col = lax.broadcasted_iota(jnp.int32, (BLOCK, BLOCK), 1)
    return row >= col if lower else row <= col


def of_head(ref, h):
    return ref[0, :, pl.ds(pl.multiple_of(h * DK, DK), DK)]


def put_head(ref, h, value, index=0):
    ref[index, :, pl.ds(pl.multiple_of(h * DK, DK), DK)] = value


def pair_of(ref, h):
    return [ref[h, 0], ref[h, 1]]


def put_pair(ref, h, terms):
    ref[h, 0], ref[h, 1] = terms


def sum_of(terms):
    return terms[0].astype(F32) + terms[1].astype(F32)


def forget_of(squashed, bound):
    return bound + (1.0 - bound) * squashed


def encode(ref, i, x, *rows):
    top = jnp.maximum(jnp.max(jnp.abs(x), axis=0, keepdims=True), 1e-36)
    top = (top * 1.01).astype(BF16).astype(F32)
    ref[i, :DK] = jnp.exp(x * (RANGE / top)).astype(BF16)
    place = lax.broadcasted_iota(jnp.int32, (EXTRA, DK), 0)
    extra = jnp.zeros((EXTRA, DK), F32)
    for r, row in enumerate((top,) + rows):
        extra = jnp.where(place == r, row, extra)
    ref[i, DK:] = extra.astype(BF16)


def decode(ref, i):
    extra = ref[i, DK:].astype(F32)
    return jnp.log(ref[i, :DK].astype(F32)) * (extra[0:1] * (1.0 / RANGE)), extra


def call(kernel, name, ins, outs, streamed=(), kept=(), scratch=()):
    hbm = pl.BlockSpec(memory_space=pltpu.HBM)
    return pl.pallas_call(
        kernel,
        out_shape=[*outs, *[pltpu.HBM(x.shape, x.dtype) for x in kept]],
        in_specs=[hbm] * len(streamed) + [VMEM] * len(ins),
        out_specs=[SMEM if x.ndim == 1 else VMEM for x in outs] + [hbm] * len(kept),
        scratch_shapes=scratch,
        compiler_params=PARAMS,
        name=name,
    )(*[pltpu.with_memory_space_constraint(x, pltpu.HBM) for x in streamed], *ins)


def buffers(*arrays):
    return [pltpu.VMEM(x.shape, x.dtype) for x in arrays] + [pltpu.SemaphoreType.DMA((len(arrays), PIECES))]


def piece_of(ref, p):
    if ref.shape[0] == 1:
        width = ref.shape[2] // PIECES
        return ref.at[:, :, pl.ds(p * width, width)]
    each = ref.shape[0] // PIECES
    return ref.at[pl.ds(p * each, each)]


def start_piece(sources, targets, sems, p):
    copies = [
        pltpu.make_async_copy(piece_of(source, p), piece_of(target, p), sems.at[a, p])
        for a, (source, target) in enumerate(zip(sources, targets))
    ]
    for copy in copies:
        copy.start()
    return copies


def start_copies(sources, targets, sems, heads):
    copies = [start_piece(sources, targets, sems, p) for p in range(PIECES)]

    def wait(h):
        if h % (heads // PIECES) == 0:
            for copy in copies[h * PIECES // heads]:
                copy.wait()

    return wait


def together(turn, heads, wait=None, after=None):
    for first in range(0, heads, GROUP):
        for h in range(first, first + GROUP):
            if wait is not None:
                wait(h)
        turns = [turn(h) for h in range(first, first + GROUP)]
        while turns:
            turns = [t for t in turns if next(t, None) is not None]
        if after is not None:
            for h in range(first, first + GROUP):
                after(h)


def own_state_kernel(
    logit_hbm, value_hbm, bound_hbm, run_ref, k_ref, own_ref, v_ref, coded_ref,
    logit_ref, value_ref, bound_ref, sems,
):
    wait = start_copies(
        (logit_hbm, value_hbm, bound_hbm), (logit_ref, value_ref, bound_ref), sems, own_ref.shape[0]
    )
    ones_below = [jnp.where(triangle(True), 1.0, 0.0).astype(BF16)]
    for h in range(own_ref.shape[0]):
        wait(h)
        bound = of_head(bound_ref, h)
        squashed = jax.nn.sigmoid(of_head(logit_ref, h).astype(F32))
        forget = forget_of(squashed, bound)
        run = product(ones_below, parts(jnp.log(forget), 2), NN)
        k_scaled = parts((1.0 - forget) * jnp.exp(-run))
        last = run[BLOCK - 1 : BLOCK]
        v = of_head(value_ref, h)
        own = product([v], k_scaled, TN)
        run_ref[h] = run
        v_ref[h] = v
        put_pair(k_ref, h, k_scaled)
        own_ref[h] = own
        encode(coded_ref, h, own * jnp.exp(last), *[term.astype(F32) for term in parts(last, 3)])


def states_before_kernel(coded_ref, out_ref, decay_ref):
    state = jnp.zeros((DK, DK), F32)
    for i in range(coded_ref.shape[0]):
        encode(out_ref, i, state)
        own, extra = decode(coded_ref, i)
        decay = jnp.exp(extra[1:2] + extra[2:3] + extra[3:4])
        decay_ref[i] = jnp.broadcast_to(decay, decay_ref.shape[1:])
        state = state * decay + own


def states_after_kernel(coded_ref, decay_ref, out_ref):
    later = jnp.zeros((DK, DK), F32)
    for i in reversed(range(coded_ref.shape[0])):
        later = later * decay_ref[i, 0:1]
        encode(out_ref, i, later)
        later = later + decode(coded_ref, i)[0]


def attended_kernel(
    query_hbm, gates_hbm, grad_hbm, gain_hbm, coded_ref, run_ref, k_ref, v_ref,
    q_ref, score_ref, pull_ref, gate_ref, att_ref, state_ref, sums_ref, go_ref,
    query_ref, gates_ref, grad_ref, gain_ref, sems,
):
    wait = start_copies(
        (query_hbm, gates_hbm, grad_hbm, gain_hbm), (query_ref, gates_ref, grad_ref, gain_ref), sems, v_ref.shape[0]
    )
    lower = triangle(True)
    go_ref[0] = 1
    totals = [jnp.zeros((BLOCK, DK), F32)] * 2

    def turn(h):
        q_scaled = parts(of_head(query_ref, h).astype(F32) * jnp.exp(run_ref[h]))
        put_pair(q_ref, h, q_scaled)
        yield True
        scores = product(q_scaled, pair_of(k_ref, h), NT)
        states = parts(decode(coded_ref, h)[0])
        put_pair(state_ref, h, states)
        yield True
        scores = parts(jnp.where(lower, scores, 0.0))
        put_pair(score_ref, h, scores)
        yield True
        attended = product(scores, [v_ref[h]], NN) + product(q_scaled, states, NT)
        gates = of_head(gates_ref, h).astype(F32)
        gated = jax.nn.sigmoid(gates)
        grad = of_head(grad_ref, h).astype(F32) * of_head(gain_ref, h)
        pull = grad * (gates * gated)
        pull_ref[h] = pull
        gate_ref[h] = grad * gated * (1.0 + gates * (1.0 - gated))
        yield True
        att_ref[h] = attended
        totals[0] = totals[0] + attended * attended
        totals[1] = totals[1] + pull * attended

    together(turn, v_ref.shape[0], wait)
    for i, total in enumerate(totals):
        sums_ref[8 * i : 8 * i + 8] = jnp.broadcast_to(jnp.sum(total.T, axis=0, keepdims=True), (8, BLOCK))


def early_grads_kernel(
    mine_ref, other_ref, att_ref, pull_ref, gate_ref, run_ref, q_ref, k_ref, v_ref, own_ref, state_ref, score_ref,
    coded_ref, grads_ref, kept_hbm, value_part_hbm, k_hbm, kept_ref, value_part_ref, sems, k_sem,
):
    heads = v_ref.shape[0]
    copies = [pltpu.make_async_copy(k_ref, k_hbm, k_sem)]
    copies[0].start()
    ones_above = [jnp.where(triangle(False), 1.0, 0.0).astype(BF16)]
    sums = mine_ref[...] + other_ref[...]
    root = jnp.sqrt(sums[0:8] / HEAD_COLUMNS + EPSILON)
    weigh = sums[8:16] / (HEAD_COLUMNS * (root * root * root))
    fill = jnp.zeros((BLOCK - 16, BLOCK), F32)
    columns = jnp.concatenate([1.0 / root, weigh, fill], axis=0).T
    over_root = jnp.broadcast_to(columns[:, 0:1], (BLOCK, DK))
    weigh = jnp.broadcast_to(columns[:, 8:9], (BLOCK, DK))
    lower = triangle(True)

    def turn(h):
        attended = att_ref[h]
        put_head(grads_ref, h, (gate_ref[h] * (attended * over_root)).astype(BF16))
        douts = parts(pull_ref[h] * over_root - attended * weigh)
        q_scaled = pair_of(q_ref, h)
        yield True
        own = product(douts, q_scaled, TN)
        pairs = product(douts, [v_ref[h]], NT)
        yield True
        encode(coded_ref, h, own)
        pairs = parts(jnp.where(lower, pairs, 0.0))
        value_part_ref[h] = product(pair_of(score_ref, h), douts, TN)
        yield True
        k_scaled = pair_of(k_ref, h)
        states = pair_of(state_ref, h)
        q_part = product(pairs, k_scaled, NN) + product(douts, states, NN)
        k_part = product(pairs, q_scaled, TN)
        yield True
        grow = jnp.exp(run_ref[h])
        shrink = jnp.exp(-run_ref[h])
        put_head(grads_ref, h, (grow * q_part).astype(BF16), 1)
        keys = sum_of(k_scaled)
        terms = parts(sum_of(q_scaled) * q_part - keys * k_part, 2)
        kept_ref[h, 1] = shrink
        kept_ref[h, 2] = sum_of(states) + own_ref[h]
        yield True
        kept_ref[h, 0] = product(ones_above, terms, NN) - (1.0 - keys * grow) * (shrink * k_part)

    def after(h):
        if (h + 1) % (heads // PIECES) == 0:
            copies.extend(
                start_piece((kept_ref, value_part_ref), (kept_hbm, value_part_hbm), sems, h * PIECES // heads)
            )

    together(turn, heads, after=after)
    for copy in copies:
        copy.wait()


def value_grad_kernel(
    value_part_hbm, k_hbm, coded_ref, first_ref, second_ref, third_ref, value_part_ref, k_ref, sems
):
    heads = k_ref.shape[0]
    wait = start_copies((value_part_hbm, k_hbm), (value_part_ref, k_ref), sems, heads)
    for h in range(heads):
        wait(h)
        v_grad = value_part_ref[h] + product(pair_of(k_ref, h), parts(decode(coded_ref, h)[0]), NT)
        start = 0
        for ref in (first_ref, second_ref, third_ref):
            count = ref.shape[2] // DK
            if start <= h < start + count:
                put_head(ref, h - start, v_grad.astype(BF16))
            start += count


def logit_grad_kernel(
    logit_hbm, value_hbm, bound_hbm, kept_hbm, coded_ref, third_ref, logit_grad_ref,
    logit_ref, value_ref, bound_ref, kept_ref, sems,
):
    heads = kept_ref.shape[0]
    logit_grad_ref[0, :, heads * DK :] = third_ref[0]
    wait = start_copies(
        (logit_hbm, value_hbm, bound_hbm, kept_hbm), (logit_ref, value_ref, bound_ref, kept_ref), sems, heads
    )
    ones_above = [jnp.where(triangle(False), 1.0, 0.0).astype(BF16)]
    for h in range(heads):
        wait(h)
        later = decode(coded_ref, h)[0]
        shrink = kept_ref[h, 1]
        bound = of_head(bound_ref, h)
        squashed = jax.nn.sigmoid(of_head(logit_ref, h).astype(F32))
        forget = forget_of(squashed, bound)
        log_later = jnp.sum(kept_ref[h, 2] * later, axis=0, keepdims=True)
        k_part = shrink * product([of_head(value_ref, h)], parts(later), NN)
        log_grad = log_later - product(ones_above, parts((1.0 - forget) * k_part, 2), NN)
        logit_grad = (kept_ref[h, 0] + log_grad) / forget - k_part
        put_head(logit_grad_ref, h, (logit_grad * (1.0 - bound) * squashed * (1.0 - squashed)).astype(BF16))


def deliver_kernel(places, *refs):
    sources, targets, sems = refs[: len(places)], refs[len(places) : -1], refs[-1]
    copies = []
    for source, place in zip(sources, places):
        for index, column, width, target, start in place:
            copies.append(
                pltpu.make_async_copy(
                    source.at[pl.ds(index, 1), :, pl.ds(column, width)],
                    targets[target].at[:, :, pl.ds(start, width)],
                    sems.at[len(copies)],
                )
            )
            copies[-1].start()
    for copy in copies:
        copy.wait()


def deliver(arrays, places, outs):
    return pl.pallas_call(
        functools.partial(deliver_kernel, places),
        out_shape=outs,
        in_specs=[VMEM] * len(arrays),
        out_specs=[pl.BlockSpec(memory_space=pltpu.HBM)] * len(outs),
        scratch_shapes=[pltpu.SemaphoreType.DMA((sum(map(len, places)),))],
        compiler_params=PARAMS,
        name="deliver",
    )(*arrays)


def to_section(x, by):
    size = lax.axis_size("pipe")
    return lax.ppermute(x, "pipe", [(i, (i + by) % size) for i in range(size)])


def exchange(x):
    return lax.all_to_all(x, "ctx", 0, 0)


def body(queries, forget_logits, values, gates, output_grad, lower_bound, norm_gain):
    heads = queries.shape[2] // DK
    whole = jax.ShapeDtypeStruct(queries.shape, BF16)
    square = jax.ShapeDtypeStruct((heads, BLOCK, DK), F32)
    pair = jax.ShapeDtypeStruct((heads, 2, BLOCK, DK), BF16)
    coded = jax.ShapeDtypeStruct((heads, DK + EXTRA, DK), BF16)
    decays = jax.ShapeDtypeStruct((heads, 8, DK), F32)
    sums = jax.ShapeDtypeStruct((16, BLOCK), F32)
    plain = jax.ShapeDtypeStruct((heads, BLOCK, DK), BF16)
    columns = heads * DK
    around, ahead, beside = [columns * share // 8 for share in SHARES]
    first, second, third, rest = [
        jax.ShapeDtypeStruct((1, BLOCK, width), BF16) for width in (around, ahead, beside, columns + beside)
    ]
    kept = jax.ShapeDtypeStruct((heads, 3, BLOCK, DK), F32)
    flag = jax.ShapeDtypeStruct((1,), jnp.int32)

    both = jax.ShapeDtypeStruct((2, BLOCK, heads * DK), BF16)
    bound, gain = lower_bound[None], norm_gain[None]

    run, k_scaled, own_state, v, sent = call(
        own_state_kernel, "own_state", [], [square, pair, square, plain, coded],
        streamed=[forget_logits, values, bound], scratch=buffers(whole, whole, bound),
    )
    sent, decay = call(states_before_kernel, "states_before", [exchange(sent)], [coded, decays])
    q_scaled, scores, pull, gate_factor, attended, states, mine, go = call(
        attended_kernel, "attended", [exchange(sent), run, k_scaled, v],
        [pair, pair, square, square, square, pair, sums, flag], streamed=[queries, gates, output_grad, gain],
        scratch=buffers(whole, whole, whole, gain),
    )
    other = lax.ppermute(mine, "tp", [(0, 1), (1, 0)])
    sent, early, kept_now, value_part, k_kept = call(
        early_grads_kernel, "early_grads",
        [mine, other, attended, pull, gate_factor, run, q_scaled, k_scaled, v, own_state, states, scores],
        [coded, both], kept=[kept, square, pair], scratch=buffers(kept, square) + [pltpu.SemaphoreType.DMA],
    )
    early = to_section(early, -1)

    def through(sent, decay):
        (sent,) = call(states_after_kernel, "states_after", [exchange(sent), decay], [coded])
        return exchange(sent)

    arrived = lax.cond(go[0] > 0, through, lambda sent, decay: sent, sent, decay)
    arrived, early = lax.optimization_barrier((arrived, early))
    first, second, third = call(
        value_grad_kernel, "value_grad", [arrived], [first, second, third], streamed=[value_part, k_kept],
        scratch=buffers(square, pair),
    )
    first = to_section(first, 1)
    second = to_section(second, -1)
    (rest,) = call(
        logit_grad_kernel, "logit_grad", [arrived, third], [rest],
        streamed=[forget_logits, values, bound, kept_now], scratch=buffers(whole, whole, bound, kept),
    )
    rest, first, second = lax.optimization_barrier((rest, first, second))
    rest = to_section(rest, -1)
    for _ in range(lax.axis_size("pipe") - 2):
        first = to_section(first, 1)
    gate_grad, query_grad = deliver([early], [((0, 0, columns, 0, 0), (1, 0, columns, 1, 0))], [whole, whole])
    logit_grad, value_grad = deliver(
        [rest, first, second],
        [
            ((0, 0, columns, 0, 0), (0, columns, beside, 1, around + ahead)),
            ((0, 0, around, 1, 0),),
            ((0, 0, ahead, 1, around),),
        ],
        [whole, whole],
    )
    return query_grad, logit_grad, value_grad, gate_grad


def solution(mesh):
    rows = P("pipe", "ctx", "tp")
    return jax.shard_map(
        body,
        mesh=mesh,
        in_specs=(rows,) * 5 + (P("pipe", "tp"),) * 2,
        out_specs=(rows,) * 4,
        check_vma=False,
    )
```

```python
import functools

import jax
import jax.numpy as jnp
from jax import lax
from jax.experimental import pallas as pl
from jax.experimental.pallas import tpu as pltpu
from jax.sharding import PartitionSpec as P

DK = 128
BLOCK = 128
HEAD_COLUMNS = 4096
EPSILON = 1e-06

F32 = jnp.float32
BF16 = jnp.bfloat16
NN = ((1,), (0,))
NT = ((1,), (1,))
TN = ((0,), (0,))
RANGE = 84.0
EXTRA = 16
PIECES = 2
GROUP = 4
SPARE = 16
SHARES = (3, 4, 1)
PARAMS = pltpu.CompilerParams(vmem_limit_bytes=24 * 1024 * 1024)
VMEM = pl.BlockSpec(memory_space=pltpu.VMEM)


def parts(x, count=2):
    if x.dtype == BF16:
        return [x]
    terms = []
    for _ in range(count - 1):
        term = x.astype(BF16)
        terms.append(term)
        x = x - term.astype(F32)
    return terms + [x.astype(BF16)]


def product(left, right, dims):
    pairs = [
        (a, b)
        for i, a in enumerate(left)
        for j, b in enumerate(right)
        if i + j < max(len(left), len(right))
    ]
    lhs = jnp.concatenate([a for a, _ in pairs], axis=dims[0][0])
    rhs = jnp.concatenate([b for _, b in pairs], axis=dims[1][0])
    return lax.dot_general(lhs, rhs, (dims, ((), ())), preferred_element_type=F32)


def triangle(lower):
    row = lax.broadcasted_iota(jnp.int32, (BLOCK, BLOCK), 0)
    col = lax.broadcasted_iota(jnp.int32, (BLOCK, BLOCK), 1)
    return row >= col if lower else row <= col


def of_head(ref, h):
    return ref[0, :, pl.ds(pl.multiple_of(h * DK, DK), DK)]


def put_head(ref, h, value, index=0):
    ref[index, :BLOCK, pl.ds(pl.multiple_of(h * DK, DK), DK)] = value


def pair_of(ref, h):
    return [ref[h, 0], ref[h, 1]]


def put_pair(ref, h, terms):
    ref[h, 0], ref[h, 1] = terms


def sum_of(terms):
    return terms[0].astype(F32) + terms[1].astype(F32)


def forget_of(squashed, bound):
    return bound + (1.0 - bound) * squashed


def encode(ref, i, x, *rows):
    top = jnp.maximum(jnp.max(jnp.abs(x), axis=0, keepdims=True), 1e-36)
    top = (top * 1.01).astype(BF16).astype(F32)
    ref[i, :DK] = jnp.exp(x * (RANGE / top)).astype(BF16)
    place = lax.broadcasted_iota(jnp.int32, (EXTRA, DK), 0)
    extra = jnp.zeros((EXTRA, DK), F32)
    for r, row in enumerate((top,) + rows):
        extra = jnp.where(place == r, row, extra)
    ref[i, DK:] = extra.astype(BF16)


def decode(ref, i):
    extra = ref[i, DK:].astype(F32)
    return jnp.log(ref[i, :DK].astype(F32)) * (extra[0:1] * (1.0 / RANGE)), extra


def call(kernel, name, ins, outs, streamed=(), kept=(), scratch=()):
    hbm = pl.BlockSpec(memory_space=pltpu.HBM)
    return pl.pallas_call(
        kernel,
        out_shape=[*outs, *[pltpu.HBM(x.shape, x.dtype) for x in kept]],
        in_specs=[hbm] * len(streamed) + [VMEM] * len(ins),
        out_specs=[VMEM] * len(outs) + [hbm] * len(kept),
        scratch_shapes=scratch,
        compiler_params=PARAMS,
        name=name,
    )(*[pltpu.with_memory_space_constraint(x, pltpu.HBM) for x in streamed], *ins)


def buffers(*arrays, pieces=PIECES):
    return [pltpu.VMEM(x.shape, x.dtype) for x in arrays] + [pltpu.SemaphoreType.DMA((len(arrays), pieces))]


def piece_of(ref, p, pieces):
    if ref.shape[0] == 1:
        width = ref.shape[2] // pieces
        return ref.at[:, :, pl.ds(p * width, width)]
    each = ref.shape[0] // pieces
    return ref.at[pl.ds(p * each, each)]


def start_piece(sources, targets, sems, p):
    pieces = sems.shape[1]
    copies = [
        pltpu.make_async_copy(piece_of(source, p, pieces), piece_of(target, p, pieces), sems.at[a, p])
        for a, (source, target) in enumerate(zip(sources, targets))
    ]
    for copy in copies:
        copy.start()
    return copies


def start_copies(sources, targets, sems, heads):
    copies = [start_piece(sources, targets, sems, p) for p in range(PIECES)]

    def wait(h):
        if h % (heads // PIECES) == 0:
            for copy in copies[h * PIECES // heads]:
                copy.wait()

    return wait


def together(turn, heads, wait=None, after=None):
    for first in range(0, heads, GROUP):
        for h in range(first, first + GROUP):
            if wait is not None:
                wait(h)
        turns = [turn(h) for h in range(first, first + GROUP)]
        while turns:
            turns = [t for t in turns if next(t, None) is not None]
        if after is not None:
            for h in range(first, first + GROUP):
                after(h)


def own_state_kernel(
    logit_hbm, value_hbm, bound_hbm, run_ref, k_ref, own_ref, v_ref, coded_ref,
    logit_ref, value_ref, bound_ref, sems,
):
    wait = start_copies(
        (logit_hbm, value_hbm, bound_hbm), (logit_ref, value_ref, bound_ref), sems, own_ref.shape[0]
    )
    ones_below = [jnp.where(triangle(True), 1.0, 0.0).astype(BF16)]
    for h in range(own_ref.shape[0]):
        wait(h)
        bound = of_head(bound_ref, h)
        squashed = jax.nn.sigmoid(of_head(logit_ref, h).astype(F32))
        forget = forget_of(squashed, bound)
        run = product(ones_below, parts(jnp.log(forget), 2), NN)
        k_scaled = parts((1.0 - forget) * jnp.exp(-run))
        last = run[BLOCK - 1 : BLOCK]
        v = of_head(value_ref, h)
        own = product([v], k_scaled, TN)
        run_ref[h] = run
        v_ref[h] = v
        put_pair(k_ref, h, k_scaled)
        own_ref[h] = own
        encode(coded_ref, h, own * jnp.exp(last), *[term.astype(F32) for term in parts(last, 3)])


def states_before_kernel(coded_ref, out_ref, decay_ref):
    state = jnp.zeros((DK, DK), F32)
    for i in range(coded_ref.shape[0]):
        encode(out_ref, i, state)
        own, extra = decode(coded_ref, i)
        decay = jnp.exp(extra[1:2] + extra[2:3] + extra[3:4])
        decay_ref[i] = jnp.broadcast_to(decay, decay_ref.shape[1:])
        state = state * decay + own


def states_after_kernel(coded_ref, decay_ref, out_ref):
    later = jnp.zeros((DK, DK), F32)
    for i in reversed(range(coded_ref.shape[0])):
        later = later * decay_ref[i, 0:1]
        encode(out_ref, i, later)
        later = later + decode(coded_ref, i)[0]


def attended_kernel(
    query_hbm, gates_hbm, grad_hbm, gain_hbm, coded_ref, run_ref, k_ref, v_ref,
    q_ref, score_ref, pull_ref, gate_ref, att_ref, state_ref, sums_ref,
    query_ref, gates_ref, grad_ref, gain_ref, sems,
):
    wait = start_copies(
        (query_hbm, gates_hbm, grad_hbm, gain_hbm), (query_ref, gates_ref, grad_ref, gain_ref), sems, v_ref.shape[0]
    )
    lower = triangle(True)
    totals = [jnp.zeros((BLOCK, DK), F32)] * 2

    def turn(h):
        q_scaled = parts(of_head(query_ref, h).astype(F32) * jnp.exp(run_ref[h]))
        put_pair(q_ref, h, q_scaled)
        yield True
        scores = product(q_scaled, pair_of(k_ref, h), NT)
        states = parts(decode(coded_ref, h)[0])
        put_pair(state_ref, h, states)
        yield True
        scores = parts(jnp.where(lower, scores, 0.0))
        put_pair(score_ref, h, scores)
        yield True
        attended = product(scores, [v_ref[h]], NN) + product(q_scaled, states, NT)
        gates = of_head(gates_ref, h).astype(F32)
        gated = jax.nn.sigmoid(gates)
        grad = of_head(grad_ref, h).astype(F32) * of_head(gain_ref, h)
        pull = grad * (gates * gated)
        pull_ref[h] = pull
        gate_ref[h] = grad * gated * (1.0 + gates * (1.0 - gated))
        yield True
        att_ref[h] = attended
        totals[0] = totals[0] + attended * attended
        totals[1] = totals[1] + pull * attended

    together(turn, v_ref.shape[0], wait)
    for i, total in enumerate(totals):
        sums_ref[8 * i : 8 * i + 8] = jnp.broadcast_to(jnp.sum(total.T, axis=0, keepdims=True), (8, BLOCK))


def early_grads_kernel(
    mine_ref, other_ref, att_ref, pull_ref, gate_ref, run_ref, q_ref, k_ref, v_ref, own_ref, state_ref, score_ref,
    coded_ref, grads_ref, kept_hbm, value_part_hbm, k_hbm, kept_ref, value_part_ref, sems, k_sem,
):
    heads = v_ref.shape[0]
    copies = [pltpu.make_async_copy(k_ref, k_hbm, k_sem)]
    copies[0].start()
    ones_above = [jnp.where(triangle(False), 1.0, 0.0).astype(BF16)]
    sums = mine_ref[...] + other_ref[...]
    root = jnp.sqrt(sums[0:8] / HEAD_COLUMNS + EPSILON)
    weigh = sums[8:16] / (HEAD_COLUMNS * (root * root * root))
    fill = jnp.zeros((BLOCK - 16, BLOCK), F32)
    columns = jnp.concatenate([1.0 / root, weigh, fill], axis=0).T
    over_root = jnp.broadcast_to(columns[:, 0:1], (BLOCK, DK))
    weigh = jnp.broadcast_to(columns[:, 8:9], (BLOCK, DK))
    lower = triangle(True)

    def turn(h):
        attended = att_ref[h]
        put_head(grads_ref, h, (gate_ref[h] * (attended * over_root)).astype(BF16))
        douts = parts(pull_ref[h] * over_root - attended * weigh)
        q_scaled = pair_of(q_ref, h)
        yield True
        own = product(douts, q_scaled, TN)
        pairs = product(douts, [v_ref[h]], NT)
        yield True
        encode(coded_ref, h, own)
        pairs = parts(jnp.where(lower, pairs, 0.0))
        value_part_ref[h] = product(pair_of(score_ref, h), douts, TN)
        yield True
        k_scaled = pair_of(k_ref, h)
        states = pair_of(state_ref, h)
        q_part = product(pairs, k_scaled, NN) + product(douts, states, NN)
        k_part = product(pairs, q_scaled, TN)
        yield True
        grow = jnp.exp(run_ref[h])
        shrink = jnp.exp(-run_ref[h])
        put_head(grads_ref, h, (grow * q_part).astype(BF16), 1)
        keys = sum_of(k_scaled)
        terms = parts(sum_of(q_scaled) * q_part - keys * k_part, 2)
        kept_ref[h, 1] = shrink
        kept_ref[h, 2] = sum_of(states) + own_ref[h]
        yield True
        kept_ref[h, 0] = product(ones_above, terms, NN) - (1.0 - keys * grow) * (shrink * k_part)

    def after(h):
        pieces = sems.shape[1]
        if (h + 1) % (heads // pieces) == 0:
            copies.extend(
                start_piece((kept_ref, value_part_ref), (kept_hbm, value_part_hbm), sems, h * pieces // heads)
            )

    grads_ref[:, BLOCK:] = jnp.zeros((2, SPARE, grads_ref.shape[2]), BF16)
    together(turn, heads, after=after)
    for copy in copies:
        copy.wait()


def value_grad_kernel(
    value_part_hbm, k_hbm, coded_ref, first_ref, second_ref, third_ref, value_part_ref, k_ref, sems
):
    heads = k_ref.shape[0]
    wait = start_copies((value_part_hbm, k_hbm), (value_part_ref, k_ref), sems, heads)
    for h in range(heads):
        wait(h)
        v_grad = value_part_ref[h] + product(pair_of(k_ref, h), parts(decode(coded_ref, h)[0]), NT)
        start = 0
        for ref in (first_ref, second_ref, third_ref):
            count = ref.shape[2] // DK
            if start <= h < start + count:
                put_head(ref, h - start, v_grad.astype(BF16))
            start += count


def logit_grad_kernel(
    logit_hbm, value_hbm, bound_hbm, kept_hbm, coded_ref, third_ref, logit_grad_ref,
    logit_ref, value_ref, bound_ref, kept_ref, sems,
):
    heads = kept_ref.shape[0]
    logit_grad_ref[0, :, heads * DK :] = third_ref[0]
    wait = start_copies(
        (logit_hbm, value_hbm, bound_hbm, kept_hbm), (logit_ref, value_ref, bound_ref, kept_ref), sems, heads
    )
    ones_above = [jnp.where(triangle(False), 1.0, 0.0).astype(BF16)]
    for h in range(heads):
        wait(h)
        later = decode(coded_ref, h)[0]
        shrink = kept_ref[h, 1]
        bound = of_head(bound_ref, h)
        squashed = jax.nn.sigmoid(of_head(logit_ref, h).astype(F32))
        forget = forget_of(squashed, bound)
        log_later = jnp.sum(kept_ref[h, 2] * later, axis=0, keepdims=True)
        k_part = shrink * product([of_head(value_ref, h)], parts(later), NN)
        log_grad = log_later - product(ones_above, parts((1.0 - forget) * k_part, 2), NN)
        logit_grad = (kept_ref[h, 0] + log_grad) / forget - k_part
        put_head(logit_grad_ref, h, (logit_grad * (1.0 - bound) * squashed * (1.0 - squashed)).astype(BF16))


def deliver_kernel(places, *refs):
    sources, targets, sems = refs[: len(places)], refs[len(places) : -1], refs[-1]
    copies = []
    for source, place in zip(sources, places):
        for index, column, width, target, start in place:
            copies.append(
                pltpu.make_async_copy(
                    source.at[pl.ds(index, 1), pl.ds(0, BLOCK), pl.ds(column, width)],
                    targets[target].at[:, :, pl.ds(start, width)],
                    sems.at[len(copies)],
                )
            )
            copies[-1].start()
    for copy in copies:
        copy.wait()


def deliver(arrays, places, outs):
    return pl.pallas_call(
        functools.partial(deliver_kernel, places),
        out_shape=outs,
        in_specs=[VMEM] * len(arrays),
        out_specs=[pl.BlockSpec(memory_space=pltpu.HBM)] * len(outs),
        scratch_shapes=[pltpu.SemaphoreType.DMA((sum(map(len, places)),))],
        compiler_params=PARAMS,
        name="deliver",
    )(*arrays)


def to_section(x, by):
    size = lax.axis_size("pipe")
    return lax.ppermute(x, "pipe", [(i, (i + by) % size) for i in range(size)])


def exchange(x):
    return lax.all_to_all(x, "ctx", 0, 0)


def body(queries, forget_logits, values, gates, output_grad, lower_bound, norm_gain):
    heads = queries.shape[2] // DK
    whole = jax.ShapeDtypeStruct(queries.shape, BF16)
    square = jax.ShapeDtypeStruct((heads, BLOCK, DK), F32)
    pair = jax.ShapeDtypeStruct((heads, 2, BLOCK, DK), BF16)
    coded = jax.ShapeDtypeStruct((heads, DK + EXTRA, DK), BF16)
    decays = jax.ShapeDtypeStruct((heads, 8, DK), F32)
    sums = jax.ShapeDtypeStruct((16, BLOCK), F32)
    plain = jax.ShapeDtypeStruct((heads, BLOCK, DK), BF16)
    columns = heads * DK
    around, ahead, beside = [columns * share // 8 for share in SHARES]
    first, second, third, rest = [
        jax.ShapeDtypeStruct((1, BLOCK, width), BF16) for width in (around, ahead, beside, columns + beside)
    ]
    kept = jax.ShapeDtypeStruct((heads, 3, BLOCK, DK), F32)

    both = jax.ShapeDtypeStruct((2, BLOCK + SPARE, heads * DK), BF16)
    bound, gain = lower_bound[None], norm_gain[None]

    run, k_scaled, own_state, v, sent = call(
        own_state_kernel, "own_state", [], [square, pair, square, plain, coded],
        streamed=[forget_logits, values, bound], scratch=buffers(whole, whole, bound),
    )
    sent, decay = call(states_before_kernel, "states_before", [exchange(sent)], [coded, decays])
    q_scaled, scores, pull, gate_factor, attended, states, mine = call(
        attended_kernel, "attended", [exchange(sent), run, k_scaled, v],
        [pair, pair, square, square, square, pair, sums], streamed=[queries, gates, output_grad, gain],
        scratch=buffers(whole, whole, whole, gain),
    )
    other = lax.ppermute(mine, "tp", [(0, 1), (1, 0)])
    sent, early, kept_now, value_part, k_kept = call(
        early_grads_kernel, "early_grads",
        [mine, other, attended, pull, gate_factor, run, q_scaled, k_scaled, v, own_state, states, scores],
        [coded, both], kept=[kept, square, pair], scratch=buffers(kept, square, pieces=4) + [pltpu.SemaphoreType.DMA],
    )
    early = to_section(early, -1)
    (sent,) = call(states_after_kernel, "states_after", [exchange(sent), decay], [coded])
    arrived = exchange(sent)
    arrived, early = lax.optimization_barrier((arrived, early))
    first, second, third = call(
        value_grad_kernel, "value_grad", [arrived], [first, second, third], streamed=[value_part, k_kept],
        scratch=buffers(square, pair),
    )
    first = to_section(first, 1)
    second = to_section(second, -1)
    (rest,) = call(
        logit_grad_kernel, "logit_grad", [arrived, third], [rest],
        streamed=[forget_logits, values, bound, kept_now], scratch=buffers(whole, whole, bound, kept),
    )
    rest, first, second = lax.optimization_barrier((rest, first, second))
    rest = to_section(rest, -1)
    for _ in range(lax.axis_size("pipe") - 2):
        first = to_section(first, 1)
    gate_grad, query_grad = deliver([early], [((0, 0, columns, 0, 0), (1, 0, columns, 1, 0))], [whole, whole])
    logit_grad, value_grad = deliver(
        [rest, first, second],
        [
            ((0, 0, columns, 0, 0), (0, columns, beside, 1, around + ahead)),
            ((0, 0, around, 1, 0),),
            ((0, 0, ahead, 1, around),),
        ],
        [whole, whole],
    )
    return query_grad, logit_grad, value_grad, gate_grad


def solution(mesh):
    rows = P("pipe", "ctx", "tp")
    return jax.shard_map(
        body,
        mesh=mesh,
        in_specs=(rows,) * 5 + (P("pipe", "tp"),) * 2,
        out_specs=(rows,) * 4,
        check_vma=False,
    )
```

```python
import functools

import jax
import jax.numpy as jnp
from jax import lax
from jax.experimental import pallas as pl
from jax.experimental.pallas import tpu as pltpu
from jax.sharding import PartitionSpec as P

DK = 128
BLOCK = 128
HEAD_COLUMNS = 4096
EPSILON = 1e-06

F32 = jnp.float32
BF16 = jnp.bfloat16
NN = ((1,), (0,))
NT = ((1,), (1,))
TN = ((0,), (0,))
RANGE = 84.0
EXTRA = 16
PIECES = 2
GROUP = 4
SPARE = 16
SHARES = (3, 4, 1)
PARAMS = pltpu.CompilerParams(vmem_limit_bytes=24 * 1024 * 1024)
VMEM = pl.BlockSpec(memory_space=pltpu.VMEM)


def parts(x, count=2):
    if x.dtype == BF16:
        return [x]
    terms = []
    for _ in range(count - 1):
        term = x.astype(BF16)
        terms.append(term)
        x = x - term.astype(F32)
    return terms + [x.astype(BF16)]


def product(left, right, dims):
    pairs = [
        (a, b)
        for i, a in enumerate(left)
        for j, b in enumerate(right)
        if i + j < max(len(left), len(right))
    ]
    lhs = jnp.concatenate([a for a, _ in pairs], axis=dims[0][0])
    rhs = jnp.concatenate([b for _, b in pairs], axis=dims[1][0])
    return lax.dot_general(lhs, rhs, (dims, ((), ())), preferred_element_type=F32)


def triangle(lower):
    row = lax.broadcasted_iota(jnp.int32, (BLOCK, BLOCK), 0)
    col = lax.broadcasted_iota(jnp.int32, (BLOCK, BLOCK), 1)
    return row >= col if lower else row <= col


def of_head(ref, h):
    return ref[0, :, pl.ds(pl.multiple_of(h * DK, DK), DK)]


def put_head(ref, h, value, index=0):
    ref[index, :BLOCK, pl.ds(pl.multiple_of(h * DK, DK), DK)] = value


def pair_of(ref, h):
    return [ref[h, 0], ref[h, 1]]


def put_pair(ref, h, terms):
    ref[h, 0], ref[h, 1] = terms


def sum_of(terms):
    return terms[0].astype(F32) + terms[1].astype(F32)


def squash(logits):
    return 1.0 / (1.0 + jnp.exp(-logits.astype(F32)))


def forget_of(squashed, bound):
    return bound + (1.0 - bound) * squashed


def encode(ref, i, x, *rows):
    top = jnp.maximum(jnp.max(jnp.abs(x), axis=0, keepdims=True), 1e-36)
    top = (top * 1.01).astype(BF16).astype(F32)
    ref[i, :DK] = jnp.exp(x * (RANGE / top)).astype(BF16)
    place = lax.broadcasted_iota(jnp.int32, (EXTRA, DK), 0)
    extra = jnp.zeros((EXTRA, DK), F32)
    for r, row in enumerate((top,) + rows):
        extra = jnp.where(place == r, row, extra)
    ref[i, DK:] = extra.astype(BF16)


def decode(ref, i):
    extra = ref[i, DK:].astype(F32)
    return jnp.log(ref[i, :DK].astype(F32)) * (extra[0:1] * (1.0 / RANGE)), extra


def call(kernel, name, ins, outs, streamed=(), kept=(), scratch=()):
    hbm = pl.BlockSpec(memory_space=pltpu.HBM)
    return pl.pallas_call(
        kernel,
        out_shape=[*outs, *[pltpu.HBM(x.shape, x.dtype) for x in kept]],
        in_specs=[hbm] * len(streamed) + [VMEM] * len(ins),
        out_specs=[VMEM] * len(outs) + [hbm] * len(kept),
        scratch_shapes=scratch,
        compiler_params=PARAMS,
        name=name,
    )(*[pltpu.with_memory_space_constraint(x, pltpu.HBM) for x in streamed], *ins)


def buffers(*arrays, pieces=PIECES):
    return [pltpu.VMEM(x.shape, x.dtype) for x in arrays] + [pltpu.SemaphoreType.DMA((len(arrays), pieces))]


def piece_of(ref, p, pieces):
    if ref.shape[0] == 1:
        width = ref.shape[2] // pieces
        return ref.at[:, :, pl.ds(p * width, width)]
    each = ref.shape[0] // pieces
    return ref.at[pl.ds(p * each, each)]


def start_piece(sources, targets, sems, p):
    pieces = sems.shape[1]
    copies = [
        pltpu.make_async_copy(piece_of(source, p, pieces), piece_of(target, p, pieces), sems.at[a, p])
        for a, (source, target) in enumerate(zip(sources, targets))
    ]
    for copy in copies:
        copy.start()
    return copies


def start_copies(sources, targets, sems, heads):
    copies = [start_piece(sources, targets, sems, p) for p in range(PIECES)]

    def wait(h):
        if h % (heads // PIECES) == 0:
            for copy in copies[h * PIECES // heads]:
                copy.wait()

    return wait


def together(turn, heads, wait=None, after=None):
    for first in range(0, heads, GROUP):
        for h in range(first, first + GROUP):
            if wait is not None:
                wait(h)
        turns = [turn(h) for h in range(first, first + GROUP)]
        while turns:
            turns = [t for t in turns if next(t, None) is not None]
        if after is not None:
            for h in range(first, first + GROUP):
                after(h)


def own_state_kernel(
    logit_hbm, value_hbm, bound_hbm, run_ref, k_ref, own_ref, v_ref, coded_ref,
    logit_ref, value_ref, bound_ref, sems,
):
    wait = start_copies(
        (logit_hbm, value_hbm, bound_hbm), (logit_ref, value_ref, bound_ref), sems, own_ref.shape[0]
    )
    ones_below = [jnp.where(triangle(True), 1.0, 0.0).astype(BF16)]
    for h in range(own_ref.shape[0]):
        wait(h)
        bound = of_head(bound_ref, h)
        squashed = squash(of_head(logit_ref, h))
        forget = forget_of(squashed, bound)
        run = product(ones_below, parts(jnp.log(forget), 2), NN)
        k_scaled = parts((1.0 - forget) * jnp.exp(-run))
        last = run[BLOCK - 1 : BLOCK]
        v = of_head(value_ref, h)
        own = product([v], k_scaled, TN)
        run_ref[h] = run
        v_ref[h] = v
        put_pair(k_ref, h, k_scaled)
        own_ref[h] = own
        encode(coded_ref, h, own * jnp.exp(last), *[term.astype(F32) for term in parts(last, 3)])


def states_before_kernel(coded_ref, out_ref, decay_ref):
    state = jnp.zeros((DK, DK), F32)
    for i in range(coded_ref.shape[0]):
        encode(out_ref, i, state)
        own, extra = decode(coded_ref, i)
        decay = jnp.exp(extra[1:2] + extra[2:3] + extra[3:4])
        decay_ref[i] = jnp.broadcast_to(decay, decay_ref.shape[1:])
        state = state * decay + own


def states_after_kernel(coded_ref, decay_ref, out_ref):
    later = jnp.zeros((DK, DK), F32)
    for i in reversed(range(coded_ref.shape[0])):
        later = later * decay_ref[i, 0:1]
        encode(out_ref, i, later)
        later = later + decode(coded_ref, i)[0]


def attended_kernel(
    query_hbm, gates_hbm, grad_hbm, gain_hbm, coded_ref, run_ref, k_ref, v_ref,
    q_ref, score_ref, pull_ref, gate_ref, att_ref, state_ref, sums_ref,
    query_ref, gates_ref, grad_ref, gain_ref, sems,
):
    wait = start_copies(
        (query_hbm, gates_hbm, grad_hbm, gain_hbm), (query_ref, gates_ref, grad_ref, gain_ref), sems, v_ref.shape[0]
    )
    lower = triangle(True)
    totals = [jnp.zeros((BLOCK, DK), F32)] * 2

    def turn(h):
        q_scaled = parts(of_head(query_ref, h).astype(F32) * jnp.exp(run_ref[h]))
        put_pair(q_ref, h, q_scaled)
        yield True
        scores = product(q_scaled, pair_of(k_ref, h), NT)
        states = parts(decode(coded_ref, h)[0])
        put_pair(state_ref, h, states)
        yield True
        scores = parts(jnp.where(lower, scores, 0.0))
        put_pair(score_ref, h, scores)
        yield True
        attended = product(scores, [v_ref[h]], NN) + product(q_scaled, states, NT)
        gates = of_head(gates_ref, h).astype(F32)
        gated = jax.nn.sigmoid(gates)
        grad = of_head(grad_ref, h).astype(F32) * of_head(gain_ref, h)
        pull = grad * (gates * gated)
        pull_ref[h] = pull
        gate_ref[h] = grad * gated * (1.0 + gates * (1.0 - gated))
        yield True
        att_ref[h] = attended
        totals[0] = totals[0] + attended * attended
        totals[1] = totals[1] + pull * attended

    together(turn, v_ref.shape[0], wait)
    for i, total in enumerate(totals):
        sums_ref[8 * i : 8 * i + 8] = jnp.broadcast_to(jnp.sum(total.T, axis=0, keepdims=True), (8, BLOCK))


def early_grads_kernel(
    mine_ref, other_ref, att_ref, pull_ref, gate_ref, run_ref, q_ref, k_ref, v_ref, own_ref, state_ref, score_ref,
    coded_ref, grads_ref, kept_hbm, value_part_hbm, k_hbm, kept_ref, value_part_ref, sems, k_sem,
):
    heads = v_ref.shape[0]
    copies = [pltpu.make_async_copy(k_ref, k_hbm, k_sem)]
    copies[0].start()
    ones_above = [jnp.where(triangle(False), 1.0, 0.0).astype(BF16)]
    sums = mine_ref[...] + other_ref[...]
    root = jnp.sqrt(sums[0:8] / HEAD_COLUMNS + EPSILON)
    weigh = sums[8:16] / (HEAD_COLUMNS * (root * root * root))
    fill = jnp.zeros((BLOCK - 16, BLOCK), F32)
    columns = jnp.concatenate([1.0 / root, weigh, fill], axis=0).T
    over_root = jnp.broadcast_to(columns[:, 0:1], (BLOCK, DK))
    weigh = jnp.broadcast_to(columns[:, 8:9], (BLOCK, DK))
    lower = triangle(True)

    def turn(h):
        attended = att_ref[h]
        put_head(grads_ref, h, (gate_ref[h] * (attended * over_root)).astype(BF16))
        douts = parts(pull_ref[h] * over_root - attended * weigh)
        q_scaled = pair_of(q_ref, h)
        yield True
        own = product(douts, q_scaled, TN)
        pairs = product(douts, [v_ref[h]], NT)
        yield True
        encode(coded_ref, h, own)
        pairs = parts(jnp.where(lower, pairs, 0.0))
        value_part_ref[h] = product(pair_of(score_ref, h), douts, TN)
        yield True
        k_scaled = pair_of(k_ref, h)
        states = pair_of(state_ref, h)
        q_part = product(pairs, k_scaled, NN) + product(douts, states, NN)
        k_part = product(pairs, q_scaled, TN)
        yield True
        grow = jnp.exp(run_ref[h])
        shrink = jnp.exp(-run_ref[h])
        put_head(grads_ref, h, (grow * q_part).astype(BF16), 1)
        keys = sum_of(k_scaled)
        terms = parts(sum_of(q_scaled) * q_part - keys * k_part, 2)
        kept_ref[h, 1] = shrink
        kept_ref[h, 2] = sum_of(states) + own_ref[h]
        yield True
        kept_ref[h, 0] = product(ones_above, terms, NN) - (1.0 - keys * grow) * (shrink * k_part)

    def after(h):
        pieces = sems.shape[1]
        if (h + 1) % (heads // pieces) == 0:
            copies.extend(
                start_piece((kept_ref, value_part_ref), (kept_hbm, value_part_hbm), sems, h * pieces // heads)
            )

    grads_ref[:, BLOCK:] = jnp.zeros((2, SPARE, grads_ref.shape[2]), BF16)
    together(turn, heads, after=after)
    for copy in copies:
        copy.wait()


def value_grad_kernel(
    value_part_hbm, k_hbm, coded_ref, first_ref, second_ref, third_ref, value_part_ref, k_ref, sems
):
    heads = k_ref.shape[0]
    wait = start_copies((value_part_hbm, k_hbm), (value_part_ref, k_ref), sems, heads)
    for h in range(heads):
        wait(h)
        v_grad = value_part_ref[h] + product(pair_of(k_ref, h), parts(decode(coded_ref, h)[0]), NT)
        start = 0
        for ref in (first_ref, second_ref, third_ref):
            count = ref.shape[2] // DK
            if start <= h < start + count:
                put_head(ref, h - start, v_grad.astype(BF16))
            start += count


def logit_grad_kernel(
    logit_hbm, value_hbm, bound_hbm, kept_hbm, coded_ref, third_ref, logit_grad_ref,
    logit_ref, value_ref, bound_ref, kept_ref, sems,
):
    heads = kept_ref.shape[0]
    logit_grad_ref[0, :, heads * DK :] = third_ref[0]
    wait = start_copies(
        (logit_hbm, value_hbm, bound_hbm, kept_hbm), (logit_ref, value_ref, bound_ref, kept_ref), sems, heads
    )
    ones_above = [jnp.where(triangle(False), 1.0, 0.0).astype(BF16)]
    for h in range(heads):
        wait(h)
        later = decode(coded_ref, h)[0]
        shrink = kept_ref[h, 1]
        bound = of_head(bound_ref, h)
        squashed = squash(of_head(logit_ref, h))
        forget = forget_of(squashed, bound)
        log_later = jnp.sum(kept_ref[h, 2] * later, axis=0, keepdims=True)
        k_part = shrink * product([of_head(value_ref, h)], parts(later), NN)
        log_grad = log_later - product(ones_above, parts((1.0 - forget) * k_part, 2), NN)
        logit_grad = (kept_ref[h, 0] + log_grad) / forget - k_part
        put_head(logit_grad_ref, h, (logit_grad * (1.0 - bound) * squashed * (1.0 - squashed)).astype(BF16))


def deliver_kernel(places, *refs):
    sources, targets, sems = refs[: len(places)], refs[len(places) : -1], refs[-1]
    copies = []
    for source, place in zip(sources, places):
        for index, column, width, target, start in place:
            copies.append(
                pltpu.make_async_copy(
                    source.at[pl.ds(index, 1), pl.ds(0, BLOCK), pl.ds(column, width)],
                    targets[target].at[:, :, pl.ds(start, width)],
                    sems.at[len(copies)],
                )
            )
            copies[-1].start()
    for copy in copies:
        copy.wait()


def deliver(arrays, places, outs):
    return pl.pallas_call(
        functools.partial(deliver_kernel, places),
        out_shape=outs,
        in_specs=[VMEM] * len(arrays),
        out_specs=[pl.BlockSpec(memory_space=pltpu.HBM)] * len(outs),
        scratch_shapes=[pltpu.SemaphoreType.DMA((sum(map(len, places)),))],
        compiler_params=PARAMS,
        name="deliver",
    )(*arrays)


def to_section(x, by):
    size = lax.axis_size("pipe")
    return lax.ppermute(x, "pipe", [(i, (i + by) % size) for i in range(size)])


def exchange(x):
    return lax.all_to_all(x, "ctx", 0, 0)


def body(queries, forget_logits, values, gates, output_grad, lower_bound, norm_gain):
    heads = queries.shape[2] // DK
    whole = jax.ShapeDtypeStruct(queries.shape, BF16)
    square = jax.ShapeDtypeStruct((heads, BLOCK, DK), F32)
    pair = jax.ShapeDtypeStruct((heads, 2, BLOCK, DK), BF16)
    coded = jax.ShapeDtypeStruct((heads, DK + EXTRA, DK), BF16)
    decays = jax.ShapeDtypeStruct((heads, 8, DK), F32)
    sums = jax.ShapeDtypeStruct((16, BLOCK), F32)
    plain = jax.ShapeDtypeStruct((heads, BLOCK, DK), BF16)
    columns = heads * DK
    around, ahead, beside = [columns * share // 8 for share in SHARES]
    first, second, third, rest = [
        jax.ShapeDtypeStruct((1, BLOCK, width), BF16) for width in (around, ahead, beside, columns + beside)
    ]
    kept = jax.ShapeDtypeStruct((heads, 3, BLOCK, DK), F32)

    both = jax.ShapeDtypeStruct((2, BLOCK + SPARE, heads * DK), BF16)
    bound, gain = lower_bound[None], norm_gain[None]

    run, k_scaled, own_state, v, sent = call(
        own_state_kernel, "own_state", [], [square, pair, square, plain, coded],
        streamed=[forget_logits, values, bound], scratch=buffers(whole, whole, bound),
    )
    sent, decay = call(states_before_kernel, "states_before", [exchange(sent)], [coded, decays])
    q_scaled, scores, pull, gate_factor, attended, states, mine = call(
        attended_kernel, "attended", [exchange(sent), run, k_scaled, v],
        [pair, pair, square, square, square, pair, sums], streamed=[queries, gates, output_grad, gain],
        scratch=buffers(whole, whole, whole, gain),
    )
    other = lax.ppermute(mine, "tp", [(0, 1), (1, 0)])
    sent, early, kept_now, value_part, k_kept = call(
        early_grads_kernel, "early_grads",
        [mine, other, attended, pull, gate_factor, run, q_scaled, k_scaled, v, own_state, states, scores],
        [coded, both], kept=[kept, square, pair], scratch=buffers(kept, square, pieces=4) + [pltpu.SemaphoreType.DMA],
    )
    early = to_section(early, -1)
    (sent,) = call(states_after_kernel, "states_after", [exchange(sent), decay], [coded])
    arrived = exchange(sent)
    arrived, early = lax.optimization_barrier((arrived, early))
    first, second, third = call(
        value_grad_kernel, "value_grad", [arrived], [first, second, third], streamed=[value_part, k_kept],
        scratch=buffers(square, pair),
    )
    first = to_section(first, 1)
    second = to_section(second, -1)
    (rest,) = call(
        logit_grad_kernel, "logit_grad", [arrived, third], [rest],
        streamed=[forget_logits, values, bound, kept_now], scratch=buffers(whole, whole, bound, kept),
    )
    first, second = lax.optimization_barrier((first, second))
    rest = to_section(rest, -1)
    for _ in range(lax.axis_size("pipe") - 2):
        first = to_section(first, 1)
    gate_grad, query_grad = deliver([early], [((0, 0, columns, 0, 0), (1, 0, columns, 1, 0))], [whole, whole])
    logit_grad, value_grad = deliver(
        [rest, first, second],
        [
            ((0, 0, columns, 0, 0), (0, columns, beside, 1, around + ahead)),
            ((0, 0, around, 1, 0),),
            ((0, 0, ahead, 1, around),),
        ],
        [whole, whole],
    )
    return query_grad, logit_grad, value_grad, gate_grad


def solution(mesh):
    rows = P("pipe", "ctx", "tp")
    return jax.shard_map(
        body,
        mesh=mesh,
        in_specs=(rows,) * 5 + (P("pipe", "tp"),) * 2,
        out_specs=(rows,) * 4,
        check_vma=False,
    )
```

```python
import functools

import jax
import jax.numpy as jnp
from jax import lax
from jax.experimental import pallas as pl
from jax.experimental.pallas import tpu as pltpu
from jax.sharding import PartitionSpec as P

DK = 128
BLOCK = 128
HEAD_COLUMNS = 4096
EPSILON = 1e-06

F32 = jnp.float32
BF16 = jnp.bfloat16
NN = ((1,), (0,))
NT = ((1,), (1,))
TN = ((0,), (0,))
RANGE = 84.0
EXTRA = 16
PIECES = 2
GROUP = 4
SPARE = 16
SHARES = (3, 4, 1)
PARAMS = pltpu.CompilerParams(vmem_limit_bytes=24 * 1024 * 1024)
VMEM = pl.BlockSpec(memory_space=pltpu.VMEM)


def parts(x, count=2):
    if x.dtype == BF16:
        return [x]
    terms = []
    for _ in range(count - 1):
        term = x.astype(BF16)
        terms.append(term)
        x = x - term.astype(F32)
    return terms + [x.astype(BF16)]


def product(left, right, dims):
    pairs = [
        (a, b)
        for i, a in enumerate(left)
        for j, b in enumerate(right)
        if i + j < max(len(left), len(right))
    ]
    lhs = jnp.concatenate([a for a, _ in pairs], axis=dims[0][0])
    rhs = jnp.concatenate([b for _, b in pairs], axis=dims[1][0])
    return lax.dot_general(lhs, rhs, (dims, ((), ())), preferred_element_type=F32)


def triangle(lower):
    row = lax.broadcasted_iota(jnp.int32, (BLOCK, BLOCK), 0)
    col = lax.broadcasted_iota(jnp.int32, (BLOCK, BLOCK), 1)
    return row >= col if lower else row <= col


def of_head(ref, h):
    return ref[0, :, pl.ds(pl.multiple_of(h * DK, DK), DK)]


def put_head(ref, h, value, index=0):
    ref[index, :BLOCK, pl.ds(pl.multiple_of(h * DK, DK), DK)] = value


def pair_of(ref, h):
    return [ref[h, 0], ref[h, 1]]


def put_pair(ref, h, terms):
    ref[h, 0], ref[h, 1] = terms


def sum_of(terms):
    return terms[0].astype(F32) + terms[1].astype(F32)


def squash(logits):
    return 1.0 / (1.0 + jnp.exp(-logits.astype(F32)))


def forget_of(squashed, bound):
    return bound + (1.0 - bound) * squashed


def encode(ref, i, x, *rows):
    top = jnp.maximum(jnp.max(jnp.abs(x), axis=0, keepdims=True), 1e-36)
    top = (top * 1.01).astype(BF16).astype(F32)
    ref[i, :DK] = jnp.exp(x * (RANGE / top)).astype(BF16)
    place = lax.broadcasted_iota(jnp.int32, (EXTRA, DK), 0)
    extra = jnp.zeros((EXTRA, DK), F32)
    for r, row in enumerate((top,) + rows):
        extra = jnp.where(place == r, row, extra)
    ref[i, DK:] = extra.astype(BF16)


def decode(ref, i):
    extra = ref[i, DK:].astype(F32)
    return jnp.log(ref[i, :DK].astype(F32)) * (extra[0:1] * (1.0 / RANGE)), extra


def call(kernel, name, ins, outs, streamed=(), kept=(), scratch=()):
    hbm = pl.BlockSpec(memory_space=pltpu.HBM)
    return pl.pallas_call(
        kernel,
        out_shape=[*outs, *[pltpu.HBM(x.shape, x.dtype) for x in kept]],
        in_specs=[hbm] * len(streamed) + [VMEM] * len(ins),
        out_specs=[VMEM] * len(outs) + [hbm] * len(kept),
        scratch_shapes=scratch,
        compiler_params=PARAMS,
        name=name,
    )(*[pltpu.with_memory_space_constraint(x, pltpu.HBM) for x in streamed], *ins)


def buffers(*arrays, pieces=PIECES):
    return [pltpu.VMEM(x.shape, x.dtype) for x in arrays] + [pltpu.SemaphoreType.DMA((len(arrays), pieces))]


def piece_of(ref, p, pieces):
    if ref.shape[0] == 1:
        width = ref.shape[2] // pieces
        return ref.at[:, :, pl.ds(p * width, width)]
    each = ref.shape[0] // pieces
    return ref.at[pl.ds(p * each, each)]


def start_piece(sources, targets, sems, p):
    pieces = sems.shape[1]
    copies = [
        pltpu.make_async_copy(piece_of(source, p, pieces), piece_of(target, p, pieces), sems.at[a, p])
        for a, (source, target) in enumerate(zip(sources, targets))
    ]
    for copy in copies:
        copy.start()
    return copies


def start_copies(sources, targets, sems, heads):
    copies = [start_piece(sources, targets, sems, p) for p in range(PIECES)]

    def wait(h):
        if h % (heads // PIECES) == 0:
            for copy in copies[h * PIECES // heads]:
                copy.wait()

    return wait


def together(turn, heads, wait=None, after=None):
    for first in range(0, heads, GROUP):
        for h in range(first, first + GROUP):
            if wait is not None:
                wait(h)
        turns = [turn(h) for h in range(first, first + GROUP)]
        while turns:
            turns = [t for t in turns if next(t, None) is not None]
        if after is not None:
            for h in range(first, first + GROUP):
                after(h)


def own_state_kernel(
    logit_hbm, value_hbm, bound_hbm, run_ref, k_ref, own_ref, v_ref, coded_ref,
    logit_ref, value_ref, bound_ref, sems,
):
    wait = start_copies(
        (logit_hbm, value_hbm, bound_hbm), (logit_ref, value_ref, bound_ref), sems, own_ref.shape[0]
    )
    ones_below = [jnp.where(triangle(True), 1.0, 0.0).astype(BF16)]
    for h in range(own_ref.shape[0]):
        wait(h)
        bound = of_head(bound_ref, h)
        squashed = squash(of_head(logit_ref, h))
        forget = forget_of(squashed, bound)
        run = product(ones_below, parts(jnp.log(forget), 2), NN)
        k_scaled = parts((1.0 - forget) * jnp.exp(-run))
        last = run[BLOCK - 1 : BLOCK]
        v = of_head(value_ref, h)
        own = product([v], k_scaled, TN)
        run_ref[h] = run
        v_ref[h] = v
        put_pair(k_ref, h, k_scaled)
        own_ref[h] = own
        encode(coded_ref, h, own * jnp.exp(last), *[term.astype(F32) for term in parts(last, 3)])


def states_before_kernel(coded_ref, out_ref, decay_ref):
    state = jnp.zeros((DK, DK), F32)
    for i in range(coded_ref.shape[0]):
        encode(out_ref, i, state)
        own, extra = decode(coded_ref, i)
        decay = jnp.exp(extra[1:2] + extra[2:3] + extra[3:4])
        decay_ref[i] = jnp.broadcast_to(decay, decay_ref.shape[1:])
        state = state * decay + own


def states_after_kernel(coded_ref, decay_ref, out_ref):
    later = jnp.zeros((DK, DK), F32)
    for i in reversed(range(coded_ref.shape[0])):
        later = later * decay_ref[i, 0:1]
        encode(out_ref, i, later)
        later = later + decode(coded_ref, i)[0]


def attended_kernel(
    query_hbm, gates_hbm, grad_hbm, gain_hbm, coded_ref, run_ref, k_ref, v_ref,
    q_ref, score_ref, pull_ref, gate_ref, att_ref, state_ref, sums_ref,
    query_ref, gates_ref, grad_ref, gain_ref, sems,
):
    wait = start_copies(
        (query_hbm, gates_hbm, grad_hbm, gain_hbm), (query_ref, gates_ref, grad_ref, gain_ref), sems, v_ref.shape[0]
    )
    lower = triangle(True)
    for h in range(v_ref.shape[0]):
        put_pair(state_ref, h, parts(decode(coded_ref, h)[0]))
    totals = [jnp.zeros((BLOCK, DK), F32)] * 2

    def turn(h):
        q_scaled = parts(of_head(query_ref, h).astype(F32) * jnp.exp(run_ref[h]))
        put_pair(q_ref, h, q_scaled)
        yield True
        scores = product(q_scaled, pair_of(k_ref, h), NT)
        states = pair_of(state_ref, h)
        yield True
        scores = parts(jnp.where(lower, scores, 0.0))
        put_pair(score_ref, h, scores)
        yield True
        attended = product(scores, [v_ref[h]], NN) + product(q_scaled, states, NT)
        gates = of_head(gates_ref, h).astype(F32)
        gated = jax.nn.sigmoid(gates)
        grad = of_head(grad_ref, h).astype(F32) * of_head(gain_ref, h)
        pull = grad * (gates * gated)
        pull_ref[h] = pull
        gate_ref[h] = grad * gated * (1.0 + gates * (1.0 - gated))
        yield True
        att_ref[h] = attended
        totals[0] = totals[0] + attended * attended
        totals[1] = totals[1] + pull * attended

    together(turn, v_ref.shape[0], wait)
    for i, total in enumerate(totals):
        sums_ref[8 * i : 8 * i + 8] = jnp.broadcast_to(jnp.sum(total.T, axis=0, keepdims=True), (8, BLOCK))


def early_grads_kernel(
    mine_ref, other_ref, att_ref, pull_ref, gate_ref, run_ref, q_ref, k_ref, v_ref, own_ref, state_ref, score_ref,
    coded_ref, grads_ref, kept_hbm, value_part_hbm, k_hbm, kept_ref, value_part_ref, sems, k_sem,
):
    heads = v_ref.shape[0]
    copies = [pltpu.make_async_copy(k_ref, k_hbm, k_sem)]
    copies[0].start()
    ones_above = [jnp.where(triangle(False), 1.0, 0.0).astype(BF16)]
    sums = mine_ref[...] + other_ref[...]
    root = jnp.sqrt(sums[0:8] / HEAD_COLUMNS + EPSILON)
    weigh = sums[8:16] / (HEAD_COLUMNS * (root * root * root))
    fill = jnp.zeros((BLOCK - 16, BLOCK), F32)
    columns = jnp.concatenate([1.0 / root, weigh, fill], axis=0).T
    over_root = jnp.broadcast_to(columns[:, 0:1], (BLOCK, DK))
    weigh = jnp.broadcast_to(columns[:, 8:9], (BLOCK, DK))
    lower = triangle(True)

    def turn(h):
        attended = att_ref[h]
        put_head(grads_ref, h, (gate_ref[h] * (attended * over_root)).astype(BF16))
        douts = parts(pull_ref[h] * over_root - attended * weigh)
        q_scaled = pair_of(q_ref, h)
        yield True
        own = product(douts, q_scaled, TN)
        pairs = product(douts, [v_ref[h]], NT)
        yield True
        encode(coded_ref, h, own)
        pairs = parts(jnp.where(lower, pairs, 0.0))
        value_part_ref[h] = product(pair_of(score_ref, h), douts, TN)
        yield True
        k_scaled = pair_of(k_ref, h)
        states = pair_of(state_ref, h)
        q_part = product(pairs, k_scaled, NN) + product(douts, states, NN)
        k_part = product(pairs, q_scaled, TN)
        yield True
        grow = jnp.exp(run_ref[h])
        shrink = jnp.exp(-run_ref[h])
        put_head(grads_ref, h, (grow * q_part).astype(BF16), 1)
        keys = sum_of(k_scaled)
        terms = parts(sum_of(q_scaled) * q_part - keys * k_part, 2)
        kept_ref[h, 1] = shrink
        kept_ref[h, 2] = sum_of(states) + own_ref[h]
        yield True
        kept_ref[h, 0] = product(ones_above, terms, NN) - (1.0 - keys * grow) * (shrink * k_part)

    def after(h):
        pieces = sems.shape[1]
        if (h + 1) % (heads // pieces) == 0:
            copies.extend(
                start_piece((kept_ref, value_part_ref), (kept_hbm, value_part_hbm), sems, h * pieces // heads)
            )

    grads_ref[:, BLOCK:] = jnp.zeros((2, SPARE, grads_ref.shape[2]), BF16)
    together(turn, heads, after=after)
    for copy in copies:
        copy.wait()


def value_grad_kernel(
    value_part_hbm, k_hbm, coded_ref, first_ref, second_ref, third_ref, later_ref, value_part_ref, k_ref, sems
):
    heads = k_ref.shape[0]
    wait = start_copies((value_part_hbm, k_hbm), (value_part_ref, k_ref), sems, heads)
    for h in range(heads):
        put_pair(later_ref, h, parts(decode(coded_ref, h)[0]))
    for h in range(heads):
        wait(h)
        v_grad = value_part_ref[h] + product(pair_of(k_ref, h), pair_of(later_ref, h), NT)
        start = 0
        for ref in (first_ref, second_ref, third_ref):
            count = ref.shape[2] // DK
            if start <= h < start + count:
                put_head(ref, h - start, v_grad.astype(BF16))
            start += count


def logit_grad_kernel(
    logit_hbm, value_hbm, bound_hbm, kept_hbm, later_ref, third_ref, logit_grad_ref,
    logit_ref, value_ref, bound_ref, kept_ref, sems,
):
    heads = kept_ref.shape[0]
    logit_grad_ref[0, :, heads * DK :] = third_ref[0]
    wait = start_copies(
        (logit_hbm, value_hbm, bound_hbm, kept_hbm), (logit_ref, value_ref, bound_ref, kept_ref), sems, heads
    )
    ones_above = [jnp.where(triangle(False), 1.0, 0.0).astype(BF16)]
    for h in range(heads):
        wait(h)
        laters = pair_of(later_ref, h)
        shrink = kept_ref[h, 1]
        bound = of_head(bound_ref, h)
        squashed = squash(of_head(logit_ref, h))
        forget = forget_of(squashed, bound)
        log_later = jnp.sum(kept_ref[h, 2] * sum_of(laters), axis=0, keepdims=True)
        k_part = shrink * product([of_head(value_ref, h)], laters, NN)
        log_grad = log_later - product(ones_above, parts((1.0 - forget) * k_part, 2), NN)
        logit_grad = (kept_ref[h, 0] + log_grad) / forget - k_part
        put_head(logit_grad_ref, h, (logit_grad * (1.0 - bound) * squashed * (1.0 - squashed)).astype(BF16))


def deliver_kernel(places, *refs):
    sources, targets, sems = refs[: len(places)], refs[len(places) : -1], refs[-1]
    copies = []
    for source, place in zip(sources, places):
        for index, column, width, target, start in place:
            copies.append(
                pltpu.make_async_copy(
                    source.at[pl.ds(index, 1), pl.ds(0, BLOCK), pl.ds(column, width)],
                    targets[target].at[:, :, pl.ds(start, width)],
                    sems.at[len(copies)],
                )
            )
            copies[-1].start()
    for copy in copies:
        copy.wait()


def deliver(arrays, places, outs):
    return pl.pallas_call(
        functools.partial(deliver_kernel, places),
        out_shape=outs,
        in_specs=[VMEM] * len(arrays),
        out_specs=[pl.BlockSpec(memory_space=pltpu.HBM)] * len(outs),
        scratch_shapes=[pltpu.SemaphoreType.DMA((sum(map(len, places)),))],
        compiler_params=PARAMS,
        name="deliver",
    )(*arrays)


def to_section(x, by):
    size = lax.axis_size("pipe")
    return lax.ppermute(x, "pipe", [(i, (i + by) % size) for i in range(size)])


def exchange(x):
    return lax.all_to_all(x, "ctx", 0, 0)


def body(queries, forget_logits, values, gates, output_grad, lower_bound, norm_gain):
    heads = queries.shape[2] // DK
    whole = jax.ShapeDtypeStruct(queries.shape, BF16)
    square = jax.ShapeDtypeStruct((heads, BLOCK, DK), F32)
    pair = jax.ShapeDtypeStruct((heads, 2, BLOCK, DK), BF16)
    coded = jax.ShapeDtypeStruct((heads, DK + EXTRA, DK), BF16)
    decays = jax.ShapeDtypeStruct((heads, 8, DK), F32)
    sums = jax.ShapeDtypeStruct((16, BLOCK), F32)
    plain = jax.ShapeDtypeStruct((heads, BLOCK, DK), BF16)
    columns = heads * DK
    around, ahead, beside = [columns * share // 8 for share in SHARES]
    first, second, third, rest = [
        jax.ShapeDtypeStruct((1, BLOCK, width), BF16) for width in (around, ahead, beside, columns + beside)
    ]
    kept = jax.ShapeDtypeStruct((heads, 3, BLOCK, DK), F32)

    both = jax.ShapeDtypeStruct((2, BLOCK + SPARE, heads * DK), BF16)
    bound, gain = lower_bound[None], norm_gain[None]

    run, k_scaled, own_state, v, sent = call(
        own_state_kernel, "own_state", [], [square, pair, square, plain, coded],
        streamed=[forget_logits, values, bound], scratch=buffers(whole, whole, bound),
    )
    sent, decay = call(states_before_kernel, "states_before", [exchange(sent)], [coded, decays])
    q_scaled, scores, pull, gate_factor, attended, states, mine = call(
        attended_kernel, "attended", [exchange(sent), run, k_scaled, v],
        [pair, pair, square, square, square, pair, sums], streamed=[queries, gates, output_grad, gain],
        scratch=buffers(whole, whole, whole, gain),
    )
    other = lax.ppermute(mine, "tp", [(0, 1), (1, 0)])
    sent, early, kept_now, value_part, k_kept = call(
        early_grads_kernel, "early_grads",
        [mine, other, attended, pull, gate_factor, run, q_scaled, k_scaled, v, own_state, states, scores],
        [coded, both], kept=[kept, square, pair], scratch=buffers(kept, square, pieces=4) + [pltpu.SemaphoreType.DMA],
    )
    early = to_section(early, -1)
    (sent,) = call(states_after_kernel, "states_after", [exchange(sent), decay], [coded])
    arrived = exchange(sent)
    arrived, early = lax.optimization_barrier((arrived, early))
    first, second, third, laters = call(
        value_grad_kernel, "value_grad", [arrived], [first, second, third, pair], streamed=[value_part, k_kept],
        scratch=buffers(square, pair),
    )
    first = to_section(first, 1)
    second = to_section(second, -1)
    (rest,) = call(
        logit_grad_kernel, "logit_grad", [laters, third], [rest],
        streamed=[forget_logits, values, bound, kept_now], scratch=buffers(whole, whole, bound, kept),
    )
    first, second = lax.optimization_barrier((first, second))
    rest = to_section(rest, -1)
    for _ in range(lax.axis_size("pipe") - 2):
        first = to_section(first, 1)
    gate_grad, query_grad = deliver([early], [((0, 0, columns, 0, 0), (1, 0, columns, 1, 0))], [whole, whole])
    logit_grad, value_grad = deliver(
        [rest, first, second],
        [
            ((0, 0, columns, 0, 0), (0, columns, beside, 1, around + ahead)),
            ((0, 0, around, 1, 0),),
            ((0, 0, ahead, 1, around),),
        ],
        [whole, whole],
    )
    return query_grad, logit_grad, value_grad, gate_grad


def solution(mesh):
    rows = P("pipe", "ctx", "tp")
    return jax.shard_map(
        body,
        mesh=mesh,
        in_specs=(rows,) * 5 + (P("pipe", "tp"),) * 2,
        out_specs=(rows,) * 4,
        check_vma=False,
    )
```
